256 devices in a mesh: expert: 64 (over z, y, core), tensor: 4 (over x).
Axes of the slice: x: 4, y: 4, z: 8, core: 2. Of those that a mesh axis runs over, the one named last changes fastest.
Arguments:
- attn_heads: bfloat16 [32768, 2048], P('expert', 'tensor'), may hold values from -6 to 6
- o_weight: bfloat16 [2048, 2048], P('tensor'), may hold values from -0.125 to 0.125
- resid: bfloat16 [32768, 2048], P(('expert', 'tensor')), may hold values from -6 to 6
- norm_gain: float32 [2048], replicated, may hold values from 0.1 to 1.9
- expert_ids: int32 [32768, 4], P(('expert', 'tensor')), may hold values from 0 to 63, all different within a row; in each aligned block of 128 rows (0 to 127, 128 to 255, ...) at most 11 rows name the same one
- combine_weights: float32 [32768, 4], P(('expert', 'tensor')), may hold values from 0.05 to 0.35
- w_gate_up: bfloat16 [64, 2, 2048, 1408], P('expert', None, None, 'tensor'), may hold values from -0.125 to 0.125
- w_down: bfloat16 [64, 1408, 2048], P('expert', 'tensor'), may hold values from -0.15625 to 0.15625
Outputs:
- layer_out: bfloat16 [32768, 2048], P(('expert', 'tensor'))
The draws below stay inside these ranges and needn't reach their ends.
Inputs may be any that keep to these rules, and one draw needn't show every extreme that they name: `expert_ids`: each row names 4 different experts. In the rows of one device (128 aligned rows) no expert is named more than 11 times, and in some device's rows one expert is named exactly 11 times.
All inputs are finite; a program needn't handle non-finite values.
Results may differ from the reference program's by a relative error of at most 0.015.
Values may be sent and summed in bfloat16 or wider, within the bound.
A program may use at most 128 MiB of HBM per device.

```python
import math
import jax
import jax.numpy as jnp
import numpy as np
from jax import lax

D = 2048
H = 16
DH = 128
FF = 1408
TOPK = 4
TOK_DEV = 128
E = 64
TOKENS = 32768
CAP = 11
N_TENSOR = 4


def levels(rng, dims, pieces, smallest, high):
    def one(dim, blocks):
        heights = jax.random.uniform(jax.random.fold_in(jax.random.fold_in(rng, 6), dim), (blocks,), jnp.float32, smallest / len(pieces), high / len(pieces))
        return jnp.repeat(jnp.exp(heights), dims[dim] // blocks).reshape((-1,) + (1,) * (len(dims) - dim - 1))

    level = one(*pieces[0])
    for cut in pieces[1:]:
        level = level * one(*cut)
    return level


def assign_block(own_key, own, number, rows, amount, top, most, skew):
    ranking = jax.random.permutation(own_key, amount)
    packed, ordinary = load_shares(amount, rows * top, most, skew, True), load_shares(amount, rows * top, most, skew, False)
    places = jnp.arange(amount)

    def named(tallies, rotation):
        used = int((tallies > 0).sum())
        fixed = max(1, used // 4)
        shifted = fixed + (places - fixed + rotation * (used - fixed)) % max(1, amount - fixed)
        return jnp.zeros((amount,), jnp.int32).at[ranking[jnp.where(places < fixed, places, shifted)]].set(jnp.asarray(tallies, jnp.int32))

    tallies = jnp.where(number % 4 == 0, named(packed, number // 4), named(ordinary, number - number // 4 - 1))
    mixed = jax.random.permutation(jax.random.fold_in(own, 3), amount)
    donor, sink = mixed[0:amount // 2 * 2:2], mixed[1:amount // 2 * 2:2]
    room = jnp.minimum(tallies[donor] - 1, most - tallies[sink]) // 2
    room = jnp.where((donor == ranking[0]) | (sink == ranking[0]) | (tallies[sink] == 0), 0, jnp.maximum(room, 0))
    shifted = jax.random.randint(jax.random.fold_in(own, 4), (amount // 2,), 0, 1 << 20) % (room + 1)
    tallies = tallies.at[donor].add(-shifted).at[sink].add(shifted)
    items = jnp.searchsorted(jnp.cumsum(tallies), jnp.arange(rows * top), side="right").astype(jnp.int32)
    grid = items.reshape(top, rows).T
    grid = grid[jax.random.permutation(jax.random.fold_in(own, 1), rows)]
    rotation = jax.random.randint(jax.random.fold_in(own, 2), (rows, 1), 0, top)
    return jnp.take_along_axis(grid, (jnp.arange(top)[None, :] + rotation) % top, axis=1)


def load_shares(number_of, total, limit, slope, full):
    portions = [(1 << 20) // math.isqrt(grade ** slope) + 1 for grade in range(1, number_of + 1)]
    largest = limit if full else min(limit, max(-(-total // number_of), total * portions[0] // sum(portions)))
    least = 1 if total - largest >= number_of - 1 else 0
    counts, rest = [largest] + [least] * (number_of - 1), total - largest - least * (number_of - 1)
    while rest > 0:
        candidates = [i for i in range(1, number_of) if counts[i] < largest] or [i for i in range(1, number_of) if counts[i] < limit]
        whole, budget = sum([portions[i] for i in candidates]), rest
        for i in candidates:
            extra = min(limit - counts[i], max(1, budget * portions[i] // whole), rest)
            counts[i] = counts[i] + extra
            rest = rest - extra
    return np.array(counts)


def scatter_about(stream_key, shape, spread, bound, split=(), kind=jnp.bfloat16):
    result = jax.random.normal(stream_key, shape, jnp.float32) * spread
    if len(split) > 0:
        result = levels(stream_key, shape, split, -0.22, 0.18) * result
    return jnp.clip(result, min=-bound, max=bound).astype(kind)


def setup_inputs(seed: int = 0) -> dict:
    key_list = jax.random.split(jax.random.key(seed), 9)
    attn_heads = scatter_about(key_list[0], (TOKENS, H * DH), 1.0, 6.0, ((0, 64), (1, 4)))
    o_weight = scatter_about(key_list[1], (H * DH, D), (H * DH) ** -0.5, 0.125, ((0, 4),))
    resid = scatter_about(key_list[2], (TOKENS, D), 1.0, 6.0, ((0, 256),))
    norm_gain = jnp.clip(1.0 + 0.18 * jax.random.normal(key_list[3], (D,), jnp.float32), 0.1, 1.9)
    expert_ids_keys = jax.random.split(jax.random.fold_in(key_list[4], 1), TOKENS // TOK_DEV)
    expert_ids_turns = jax.random.permutation(jax.random.fold_in(key_list[4], 3), TOKENS // TOK_DEV)
    expert_ids = jax.vmap(lambda own, number: assign_block(jax.random.fold_in(key_list[4], 2), own, number, TOK_DEV, E, TOPK, CAP, 2))(expert_ids_keys, expert_ids_turns).reshape((TOKENS, TOPK))
    combine_weights = jnp.clip(0.05 + 0.29999999 * jax.random.uniform(key_list[5], (TOKENS, TOPK), jnp.float32) ** levels(key_list[5], (TOKENS, TOPK), ((0, 256),), -0.2, 0.2), 0.05, 0.35)
    w_gate_up = scatter_about(key_list[6], (E, 2, D, FF), D ** -0.5, 0.125, ((0, 64), (3, 4)))
    w_down = scatter_about(key_list[7], (E, FF, D), FF ** -0.5, 0.15625, ((0, 64), (1, 4)))
    return {"attn_heads": attn_heads, "o_weight": o_weight, "resid": resid, "norm_gain": norm_gain, "expert_ids": expert_ids, "combine_weights": combine_weights, "w_gate_up": w_gate_up, "w_down": w_down}


eps_norm = 1e-06

def swiglu(inputs, gate_cols, up_cols):
    gate_val = jnp.dot(inputs, gate_cols, preferred_element_type=jnp.float32)
    up_value = jnp.dot(inputs, up_cols, preferred_element_type=jnp.float32)
    return (jax.nn.silu(gate_val) * up_value).astype(jnp.bfloat16)

def reference(attn_heads, o_weight, resid, norm_gain, expert_ids, combine_weights, w_gate_up, w_down):
    attn_out = jnp.dot(attn_heads, o_weight, preferred_element_type=jnp.float32)
    mixed = resid.astype(jnp.float32) + attn_out
    scale = lax.rsqrt(lax.optimization_barrier(jnp.mean(mixed * mixed, axis=1, keepdims=True)) + eps_norm)
    normed = (mixed * scale * norm_gain[None, :]).astype(jnp.bfloat16)
    num_blocks = TOKENS // TOK_DEV
    pair_expert = expert_ids.reshape(num_blocks, TOK_DEV * TOPK)
    onehot = (pair_expert[:, :, None] == jnp.arange(E, dtype=jnp.int32)[None, None, :]).astype(jnp.int32)
    slot_rank = lax.optimization_barrier(jnp.sum((jnp.cumsum(onehot, axis=1) - onehot) * onehot, axis=2))
    block_base = (jnp.arange(num_blocks, dtype=jnp.int32) * CAP)[:, None]
    slot_index = (pair_expert * (num_blocks * CAP) + block_base + slot_rank).reshape(-1).astype(jnp.int32)
    pair_count = TOKENS * TOPK
    table = jnp.full((E * num_blocks * CAP,), pair_count, jnp.int32)
    table = table.at[slot_index].set(jnp.arange(pair_count, dtype=jnp.int32))
    table = table.reshape(E, num_blocks * CAP)
    normed_pad = jnp.concatenate([normed, jnp.zeros((1, D), jnp.bfloat16)], axis=0)
    weight_pad = jnp.concatenate([combine_weights.reshape(-1), jnp.zeros((1,), jnp.float32)])
    block_width = FF // N_TENSOR

    def expert_step(accum, inputs):
        pair_rows, gate_up, down_rows = inputs
        token_of = (pair_rows // TOPK).astype(jnp.int32)
        slot_rows = normed_pad[token_of]
        hidden = swiglu(slot_rows, gate_up[0], gate_up[1])
        total = jnp.zeros((slot_rows.shape[0], D), jnp.float32)
        for block_index in range(N_TENSOR):
            offset = block_index * block_width
            partial_sum = jnp.dot(hidden[:, offset:offset + block_width], down_rows[offset:offset + block_width], preferred_element_type=jnp.float32)
            total = total + lax.optimization_barrier(partial_sum.astype(jnp.bfloat16)).astype(jnp.float32)
        results = total.astype(jnp.bfloat16)
        accum = accum.at[token_of].add(weight_pad[pair_rows][:, None] * results.astype(jnp.float32))
        return (accum, None)
    accum = jnp.zeros((TOKENS + 1, D), jnp.float32)
    accum = lax.scan(expert_step, accum, (table, w_gate_up, w_down))[0]
    return (mixed + accum[:TOKENS]).astype(jnp.bfloat16)
```

```python
import jax
import jax.numpy as jnp
from jax import lax
from jax.sharding import PartitionSpec as P

eps_norm = 1e-06


def on_device(
    attn_heads, o_weight, resid, norm_gain, expert_ids, combine_weights, w_gate_up, w_down
):
    tok_rows, width = resid.shape
    top_count = expert_ids.shape[1]
    num_experts = w_gate_up.shape[0] * lax.axis_size("expert")
    capacity = max(
        2, min(tok_rows, (4 * tok_rows * top_count + 3 * num_experts - 1) // (3 * num_experts))
    )
    partial = jnp.dot(attn_heads, o_weight, preferred_element_type=jnp.float32).astype(jnp.bfloat16)
    attn_out = lax.psum_scatter(partial, "tensor", scatter_dimension=0, tiled=True)
    gate_up_all = lax.all_gather(jnp.swapaxes(w_gate_up[0], 1, 2), "tensor", axis=0)
    down_all = lax.all_gather(w_down[0], "tensor", axis=0, tiled=True)
    mixed = resid.astype(jnp.float32) + attn_out.astype(jnp.float32)
    scale = lax.rsqrt(jnp.mean(mixed * mixed, axis=1, keepdims=True) + eps_norm)
    normed = (mixed * scale * norm_gain[None, :]).astype(jnp.bfloat16)

    named = expert_ids[:, :, None] == jnp.arange(num_experts, dtype=jnp.int32)[None, None, :]
    holds = jnp.any(named, axis=1)
    row = jnp.arange(tok_rows, dtype=jnp.int32)
    earlier = (row[None, :] < row[:, None]).astype(jnp.bfloat16)
    rank = jnp.dot(earlier, holds.astype(jnp.bfloat16), preferred_element_type=jnp.float32)
    rank = jnp.where(holds, rank.astype(jnp.int32), -1)
    weight = jnp.sum(jnp.where(named, combine_weights[:, :, None], 0.0), axis=1)
    slot = jnp.arange(capacity, dtype=jnp.int32)
    place = rank[:, :, None] == slot[None, None, :]
    pick = place.astype(jnp.bfloat16).reshape(tok_rows, num_experts * capacity)
    outgoing = lax.dot_general(
        pick, normed, (((0,), (0,)), ((), ())), preferred_element_type=jnp.float32
    ).astype(jnp.bfloat16)
    received = lax.all_to_all(
        outgoing.reshape(num_experts, capacity, width), "expert", split_axis=0, concat_axis=0, tiled=True
    ).reshape(-1, width)
    total = jnp.zeros(received.shape, jnp.float32)
    gate = lax.dot_general(
        received, gate_up_all[:, 0].reshape(-1, width), (((1,), (1,)), ((), ())),
        preferred_element_type=jnp.float32,
    )
    up = lax.dot_general(
        received, gate_up_all[:, 1].reshape(-1, width), (((1,), (1,)), ((), ())),
        preferred_element_type=jnp.float32,
    )
    hidden = (jax.nn.silu(gate) * up).astype(jnp.bfloat16)
    total = jnp.dot(hidden, down_all, preferred_element_type=jnp.float32).astype(jnp.bfloat16)
    returned = lax.all_to_all(
        total.reshape(num_experts, capacity, width), "expert", split_axis=0, concat_axis=0, tiled=True
    ).reshape(-1, width)
    spread = jnp.where(place, weight[:, :, None], 0.0).reshape(tok_rows, num_experts * capacity)
    high = spread.astype(jnp.bfloat16)
    low = (spread - high.astype(jnp.float32)).astype(jnp.bfloat16)
    moe_out = jnp.dot(high, returned, preferred_element_type=jnp.float32) + jnp.dot(
        low, returned, preferred_element_type=jnp.float32
    )
    return (mixed + moe_out).astype(jnp.bfloat16)


def solution(mesh):
    in_specs = (
        P("expert", "tensor"),
        P("tensor", None),
        P(("expert", "tensor"), None),
        P(),
        P(("expert", "tensor"), None),
        P(("expert", "tensor"), None),
        P("expert", None, None, "tensor"),
        P("expert", "tensor", None),
    )
    out_specs = P(("expert", "tensor"), None)
    return jax.shard_map(
        on_device, mesh=mesh, in_specs=in_specs, out_specs=out_specs, check_vma=False
    )
```

```python
import functools

import jax
import jax.numpy as jnp
from jax import lax
from jax.experimental import pallas as pl
from jax.experimental.pallas import tpu as pltpu
from jax.sharding import PartitionSpec as P

MESH = pl.DeviceIdType.MESH
BF16 = jnp.bfloat16
F32 = jnp.float32
eps_norm = 1e-06

NZ, NY, NC, NX = 8, 4, 2, 4
GROUP = NY * NC
TOK = 128
D = 2048
CAP = 11
PIECE = 96
ROWS = GROUP * PIECE
HID = 352
NQ = 4
DQ = D // NQ
TILE = 384
PACE = 2


def nt(a, b):
    return lax.dot_general(a, b, (((1,), (1,)), ((), ())), preferred_element_type=F32)


def mm(a, b):
    return jnp.dot(a, b, preferred_element_type=F32)


def cols(q):
    return pl.ds(q * DQ, DQ)


def kernel(
    attn, ow, resid, gain, ids, wts, wgu_in, wd_in, out,
    mixed, far, nbr, far_in, nbr_in, meta_out, meta, vrow, gather, comb, gw,
    tok, ysend, yrecv, xrecv, xback, yback, zrecv, wgu, wd, acc, hidden,
    wl_sem, ws_sem, wr_sem, fs_sem, fr_sem, ns_sem, nr_sem, ms_sem, mr_sem,
    as_sem, ar_sem, ys_sem, yr_sem, xs_sem, xr_sem, bs_sem, br_sem, cs_sem, cr_sem, zs_sem, zr_sem,
):
    e = lax.axis_index("expert")
    x = lax.axis_index("tensor")
    z = e // GROUP
    y = (e // NC) % NY
    c = e % NC
    own_d = e % GROUP
    xr, xl = (x + 1) % NX, (x + NX - 1) % NX
    flip = x + 1 - 2 * (x % 2)
    mirror = NX - 1 - x
    wx = (1 - c) * mirror + c * flip
    px = (1 - c) * flip + c * mirror

    def at_z(dz):
        return (((z + dz + NZ) % NZ) * GROUP + own_d, x)

    def at_yc(j):
        return (z * GROUP + ((y + j // NC) % NY) * NC + (c + j % NC) % NC, x)

    def d_from(j):
        return ((y + NY - j // NC) % NY) * NC + (c + j % NC) % NC

    def d_to(j):
        return ((y + j // NC) % NY) * NC + (c + j % NC) % NC

    def rcopy(src, dst, send, recv, dev):
        return pltpu.make_async_remote_copy(
            src_ref=src, dst_ref=dst, send_sem=send, recv_sem=recv, device_id=dev, device_id_type=MESH
        )

    def landed(ref, sem):
        pltpu.make_async_copy(ref, ref, sem).wait()

    wloc = [
        pltpu.make_async_copy(wgu_in.at[0], wgu.at[0, pl.ds(0, HID)], wl_sem.at[0]),
        pltpu.make_async_copy(wgu_in.at[1], wgu.at[1, pl.ds(0, HID)], wl_sem.at[1]),
        pltpu.make_async_copy(wd_in, wd.at[pl.ds(0, HID)], wl_sem.at[2]),
    ]
    for copy in wloc:
        copy.start()

    barrier = pltpu.get_barrier_semaphore()
    peers = [at_z(k) for k in range(1, NZ)] + [at_yc(j) for j in range(1, GROUP)] + [(e, xr), (e, xl)]
    for dev in peers:
        pl.semaphore_signal(barrier, inc=1, device_id=dev, device_id_type=MESH)
    pl.semaphore_wait(barrier, len(peers))

    half = D // 2

    def project(owner, q):
        return mm(attn[pl.ds(pl.multiple_of(owner * TOK, TOK), TOK), :], ow[:, cols(q)])

    opposite = (x + 2) % NX
    far_copy = []
    for side in range(2):
        for q in (2 * side, 2 * side + 1):
            far[side, :, pl.ds((q % 2) * DQ, DQ)] = project(opposite, q).astype(BF16)
        far_copy.append(
            rcopy(far.at[side], far_in.at[side], fs_sem.at[side], fr_sem.at[side], (e, (xr, xl)[side]))
        )
        far_copy[-1].start()
    nbr_copy = []
    for side in range(2):
        part = 1 - side
        for q in (2 * part, 2 * part + 1):
            nbr[side, part, :, pl.ds((q % 2) * DQ, DQ)] = project((xr, xl)[side], q).astype(BF16)
        nbr_copy.append(
            rcopy(nbr.at[side, part], nbr_in.at[side, part], ns_sem.at[side, part], nr_sem.at[side, part], (e, (xr, xl)[side]))
        )
        nbr_copy[-1].start()
    for side in range(2):
        part = side
        for q in (2 * part, 2 * part + 1):
            mixed[:, cols(q)] = project((xr, xl)[side], q)
        landed(far_in.at[side], fr_sem.at[side])
        for q in (2 * part, 2 * part + 1):
            at = pl.ds((q % 2) * DQ, DQ)
            nbr[side, part, :, at] = (mixed[:, cols(q)] + far_in[side, :, at].astype(F32)).astype(BF16)
        nbr_copy.append(
            rcopy(nbr.at[side, part], nbr_in.at[side, part], ns_sem.at[side, part], nr_sem.at[side, part], (e, (xr, xl)[side]))
        )
        nbr_copy[-1].start()
    for q in range(NQ):
        mixed[:, cols(q)] = project(x, q) + resid[:, cols(q)].astype(F32)

    expert = lax.broadcasted_iota(jnp.int32, (NZ * GROUP, TOK), 0)
    holds = jnp.zeros((NZ * GROUP, TOK), F32)
    weight = jnp.zeros((NZ * GROUP, TOK), F32)
    for k in range(ids.shape[0]):
        named = expert == ids[k : k + 1, :]
        holds = holds + jnp.where(named, 1.0, 0.0)
        weight = weight + jnp.where(named, wts[k : k + 1, :], 0.0)
    before = lax.broadcasted_iota(jnp.int32, (TOK, TOK), 0) < lax.broadcasted_iota(jnp.int32, (TOK, TOK), 1)
    rank = mm(holds.astype(BF16), jnp.where(before, 1.0, 0.0).astype(BF16))
    place = jnp.where(holds > 0.5, rank + (z * CAP).astype(F32), -1.0)
    for p in range(NZ):
        meta_out[p, 0:GROUP, :] = place[p * GROUP : (p + 1) * GROUP, :]
        meta_out[p, GROUP : 2 * GROUP, :] = weight[p * GROUP : (p + 1) * GROUP, :]
    meta_copy = []
    for k in range(1, NZ):
        to = (z + k) % NZ
        meta_copy.append(rcopy(meta_out.at[to], meta.at[z], ms_sem.at[k], mr_sem.at[k], at_z(k)))
        meta_copy[-1].start()
    meta[z] = meta_out[z]

    for side in range(2):
        for part in range(2):
            landed(nbr_in.at[side, part], nr_sem.at[side, part])
            for q in (2 * part, 2 * part + 1):
                mixed[:, cols(q)] = mixed[:, cols(q)] + nbr_in[side, part, :, pl.ds((q % 2) * DQ, DQ)].astype(F32)

    wrem = [
        rcopy(wgu_in.at[0], wgu.at[0, pl.ds(HID, HID)], ws_sem.at[0], wr_sem.at[0], (e, wx)),
        rcopy(wgu_in.at[1], wgu.at[1, pl.ds(HID, HID)], ws_sem.at[1], wr_sem.at[1], (e, wx)),
        rcopy(wd_in, wd.at[pl.ds(HID, HID)], ws_sem.at[2], wr_sem.at[2], (e, wx)),
    ]
    for copy in wrem:
        copy.start()

    square = jnp.zeros((TOK, 1), F32)
    for q in range(NQ):
        part = mixed[:, cols(q)]
        square = square + jnp.sum(part * part, axis=1, keepdims=True)
    scale = lax.rsqrt(square * (1.0 / D) + eps_norm)

    def hops(q):
        return (4, 3) if q % 2 == 0 else (3, 4)

    def block(s):
        return pl.ds(pl.multiple_of(s * TOK, TOK), TOK)

    sent = {}

    def ag_send(q, side, k):
        s = (z + NZ - (k - 1)) % NZ if side == 0 else (z + k - 1) % NZ
        ref = tok.at[q, block(s)]
        copy = rcopy(ref, ref, as_sem.at[q, side, k - 1], ar_sem.at[q, side, k - 1], at_z(1 if side == 0 else -1))
        copy.start()
        sent.setdefault(("ag", q), []).append(copy)

    def ag_start(q):
        tok[q, block(z), :] = (mixed[:, cols(q)] * scale * gain[:, cols(q)]).astype(BF16)
        for side in range(2):
            ag_send(q, side, 1)

    def ag_step(q, k):
        for side in range(2):
            if k > hops(q)[side]:
                continue
            s = (z + NZ - k) % NZ if side == 0 else (z + k) % NZ
            landed(tok.at[q, block(s)], ar_sem.at[q, side, k - 1])
            if k < hops(q)[side]:
                ag_send(q, side, k + 1)

    def piece(d):
        return pl.ds(pl.multiple_of(d * PIECE, 32), PIECE)

    def gather_step(q):
        def one(i, _):
            at = pl.ds(pl.multiple_of(i * TILE, TILE), TILE)
            ysend[q, at, :] = mm(gather[at, :], tok[q]).astype(BF16)
            return 0

        lax.fori_loop(0, ROWS // TILE, one, 0)
        for j in range(GROUP - 1, 0, -1):
            copy = rcopy(
                ysend.at[q, piece(d_to(j))], yrecv.at[q, piece(own_d)], ys_sem.at[q, j], yr_sem.at[q, j], at_yc(j)
            )
            copy.start()
            sent.setdefault(("y", q), []).append(copy)
        yrecv[q, piece(own_d), :] = ysend[q, piece(own_d), :]

    def share_step(q):
        for j in range(1, GROUP):
            landed(yrecv.at[q, piece(d_from(j))], yr_sem.at[q, j])
        copy = rcopy(yrecv.at[q], xrecv.at[q], xs_sem.at[q], xr_sem.at[q], (e, px))
        copy.start()
        sent[("x", q)] = [copy]

    def hidden_step(q, who):
        if q == 0 and who == 0:
            for copy in wloc:
                copy.wait()
            for i in range(2):
                landed(wgu.at[i, pl.ds(HID, HID)], wr_sem.at[i])
            landed(wd.at[pl.ds(HID, HID)], wr_sem.at[2])
        if who == 1:
            landed(xrecv.at[q], xr_sem.at[q])
        rows = (yrecv, xrecv)[who]

        def one(i, _):
            at = pl.ds(pl.multiple_of(i * TILE, TILE), TILE)
            to = pl.ds(pl.multiple_of(i * TILE + who * ROWS, TILE), TILE)
            lhs = rows[q, at, :]
            gate = nt(lhs, wgu[0, :, cols(q)])
            up = nt(lhs, wgu[1, :, cols(q)])
            if q > 0:
                gate = gate + acc[0, to, :]
                up = up + acc[1, to, :]
            if q < NQ - 1:
                acc[0, to, :] = gate
                acc[1, to, :] = up
            else:
                hidden[to, :] = (gate / (1.0 + jnp.exp(-gate)) * up).astype(BF16)
            return 0

        lax.fori_loop(0, ROWS // TILE, one, 0)

    def masks():
        for k in range(1, NZ):
            landed(meta.at[(z + NZ - k) % NZ], mr_sem.at[k])
        slot = lax.broadcasted_iota(jnp.int32, (PIECE, TOK), 0).astype(F32)
        eye = jnp.where(
            lax.broadcasted_iota(jnp.int32, (TOK, TOK), 0) == lax.broadcasted_iota(jnp.int32, (TOK, TOK), 1), 1.0, 0.0
        ).astype(BF16)
        for s in range(NZ):
            for d in range(GROUP):
                taken = slot == meta[s, d : d + 1, :]
                gather[d * PIECE : (d + 1) * PIECE, s * TOK : (s + 1) * TOK] = jnp.where(taken, 1.0, 0.0).astype(BF16)
                gw[d * PIECE : (d + 1) * PIECE, :] = jnp.where(
                    taken, meta[s, GROUP + d : GROUP + d + 1, :], 0.0
                ).astype(BF16)
            comb[s * TOK : (s + 1) * TOK, :] = nt(eye, gw[...]).astype(BF16)

    tasks = []
    for q in range(NQ):
        t = q * PACE
        tasks.append((t, 0, functools.partial(ag_start, q)))
        for k in range(1, 5):
            tasks.append((t + k, 1, functools.partial(ag_step, q, k)))
        tasks.append((t + 4, 2, functools.partial(gather_step, q)))
        tasks.append((t + 7, 3, functools.partial(share_step, q)))
        tasks.append((t + 7, 4, functools.partial(hidden_step, q, 0)))
        tasks.append((t + 10, 5, functools.partial(hidden_step, q, 1)))
    tasks.append((0, 9, masks))
    for task in sorted(tasks, key=lambda task: task[:2]):
        task[2]()

    def down_step(q):
        for copy in sent[("x", q)]:
            copy.wait_send()

        def one(who):
            def body(i, _):
                at = pl.ds(pl.multiple_of(i * TILE, TILE), TILE)
                of = pl.ds(pl.multiple_of(i * TILE + who * ROWS, TILE), TILE)
                (yrecv, xrecv)[who][q, at, :] = mm(hidden[of, :], wd[:, cols(q)]).astype(BF16)
                return 0

            lax.fori_loop(0, ROWS // TILE, body, 0)

        one(1)
        copy = rcopy(xrecv.at[q], xback.at[q], bs_sem.at[q], br_sem.at[q], (e, px))
        copy.start()
        sent[("b", q)] = [copy]
        one(0)

    def sum_step(q):
        landed(xback.at[q], br_sem.at[q])
        for copy in sent[("y", q)]:
            copy.wait_send()
        ysend[q] = (yrecv[q].astype(F32) + xback[q].astype(F32)).astype(BF16)
        for j in range(GROUP - 1, 0, -1):
            copy = rcopy(
                ysend.at[q, piece(d_to(j))], yback.at[q, piece(own_d)], cs_sem.at[q, j], cr_sem.at[q, j], at_yc(j)
            )
            copy.start()
            sent.setdefault(("c", q), []).append(copy)
        yback[q, piece(own_d), :] = ysend[q, piece(own_d), :]

    def rs_send(q, side, j):
        far_hops = hops(q)[side]
        k = far_hops + 1 - j
        s = (z + k) % NZ if side == 0 else (z + NZ - k) % NZ
        copy = rcopy(
            tok.at[q, block(s)], zrecv.at[q, side, j - 1], zs_sem.at[q, side, j - 1], zr_sem.at[q, side, j - 1],
            at_z(1 if side == 0 else -1),
        )
        copy.start()
        sent.setdefault(("z", q), []).append(copy)

    def combine_step(q):
        for j in range(1, GROUP):
            landed(yback.at[q, piece(d_from(j))], cr_sem.at[q, j])
        for copy in sent[("ag", q)]:
            copy.wait_send()

        def one(i, _):
            at = pl.ds(pl.multiple_of(i * 256, 256), 256)
            tok[q, at, :] = mm(comb[at, :], yback[q]).astype(BF16)
            return 0

        lax.fori_loop(0, NZ * TOK // 256, one, 0)
        for side in range(2):
            rs_send(q, side, 1)

    def rs_step(q, j):
        for side in range(2):
            far_hops = hops(q)[side]
            if j > far_hops:
                continue
            landed(zrecv.at[q, side, j - 1], zr_sem.at[q, side, j - 1])
            if j == far_hops:
                mixed[:, cols(q)] = mixed[:, cols(q)] + zrecv[q, side, j - 1].astype(F32)
                continue
            k = far_hops - j
            s = (z + k) % NZ if side == 0 else (z + NZ - k) % NZ
            tok[q, block(s), :] = (tok[q, block(s), :].astype(F32) + zrecv[q, side, j - 1].astype(F32)).astype(BF16)
            rs_send(q, side, j + 1)

    def finish(q):
        out[:, cols(q)] = (mixed[:, cols(q)] + tok[q, block(z), :].astype(F32)).astype(BF16)

    tasks = []
    for q in range(NQ):
        t = q * PACE
        tasks.append((q, 0, functools.partial(down_step, q)))
        tasks.append((t + 4, 1, functools.partial(sum_step, q)))
        tasks.append((t + 7, 2, functools.partial(combine_step, q)))
        for j in range(1, 5):
            tasks.append((t + 7 + j, 3, functools.partial(rs_step, q, j)))
        tasks.append((t + 11, 4, functools.partial(finish, q)))
    for task in sorted(tasks, key=lambda task: task[:2]):
        task[2]()

    for copy in far_copy + nbr_copy + meta_copy + wrem:
        copy.wait_send()
    for q in range(NQ):
        for kind in ("b", "c", "z"):
            for copy in sent[(kind, q)]:
                copy.wait_send()


def on_device(
    attn_heads, o_weight, resid, norm_gain, expert_ids, combine_weights, w_gate_up, w_down
):
    vmem = pl.BlockSpec(memory_space=pltpu.VMEM)
    hbm = pl.BlockSpec(memory_space=pl.ANY)
    dma = pltpu.SemaphoreType.DMA
    return pl.pallas_call(
        kernel,
        out_shape=jax.ShapeDtypeStruct((TOK, D), BF16),
        in_specs=[vmem] * 6 + [hbm] * 2,
        out_specs=vmem,
        scratch_shapes=[
            pltpu.VMEM((TOK, D), F32),
            pltpu.VMEM((2, TOK, D // 2), BF16),
            pltpu.VMEM((2, 2, TOK, D // 2), BF16),
            pltpu.VMEM((2, TOK, D // 2), BF16),
            pltpu.VMEM((2, 2, TOK, D // 2), BF16),
            pltpu.VMEM((NZ, 2 * GROUP, TOK), F32),
            pltpu.VMEM((NZ, 2 * GROUP, TOK), F32),
            pltpu.VMEM((8, TOK), F32),
            pltpu.VMEM((ROWS, NZ * TOK), BF16),
            pltpu.VMEM((NZ * TOK, ROWS), BF16),
            pltpu.VMEM((ROWS, TOK), BF16),
            pltpu.VMEM((NQ, NZ * TOK, DQ), BF16),
            pltpu.VMEM((NQ, ROWS, DQ), BF16),
            pltpu.VMEM((NQ, ROWS, DQ), BF16),
            pltpu.VMEM((NQ, ROWS, DQ), BF16),
            pltpu.VMEM((NQ, ROWS, DQ), BF16),
            pltpu.VMEM((NQ, ROWS, DQ), BF16),
            pltpu.VMEM((NQ, 2, 4, TOK, DQ), BF16),
            pltpu.VMEM((2, 2 * HID, D), BF16),
            pltpu.VMEM((2 * HID, D), BF16),
            pltpu.VMEM((2, 2 * ROWS, 2 * HID), F32),
            pltpu.VMEM((2 * ROWS, 2 * HID), BF16),
            dma((3,)), dma((3,)), dma((3,)),
            dma((2,)), dma((2,)), dma((2, 2)), dma((2, 2)), dma((NZ,)), dma((NZ,)),
            dma((NQ, 2, 4)), dma((NQ, 2, 4)), dma((NQ, GROUP)), dma((NQ, GROUP)), dma((NQ,)), dma((NQ,)),
            dma((NQ,)), dma((NQ,)), dma((NQ, GROUP)), dma((NQ, GROUP)), dma((NQ, 2, 4)), dma((NQ, 2, 4)),
        ],
        compiler_params=pltpu.CompilerParams(
            collective_id=0, has_side_effects=True, vmem_limit_bytes=60 * 2**20
        ),
        cost_estimate=pl.CostEstimate(flops=16 * 10**9, bytes_accessed=10**7, transcendentals=10**6),
    )(
        attn_heads, o_weight, resid, norm_gain[None, :], expert_ids.T, combine_weights.T,
        jnp.swapaxes(w_gate_up[0], 1, 2), w_down[0],
    )


def solution(mesh):
    in_specs = (
        P("expert", "tensor"),
        P("tensor", None),
        P(("expert", "tensor"), None),
        P(),
        P(("expert", "tensor"), None),
        P(("expert", "tensor"), None),
        P("expert", None, None, "tensor"),
        P("expert", "tensor", None),
    )
    out_specs = P(("expert", "tensor"), None)
    return jax.shard_map(
        on_device, mesh=mesh, in_specs=in_specs, out_specs=out_specs, check_vma=False
    )
```

```python
import functools

import jax
import jax.numpy as jnp
from jax import lax
from jax.experimental import pallas as pl
from jax.experimental.pallas import tpu as pltpu
from jax.sharding import PartitionSpec as P

MESH = pl.DeviceIdType.MESH
BF16 = jnp.bfloat16
F32 = jnp.float32
eps_norm = 1e-06

NZ, NY, NC, NX = 8, 4, 2, 4
GROUP = NY * NC
TOK = 128
D = 2048
CAP = 11
PIECE = 96
ROWS = GROUP * PIECE
HID = 352
NQ = 8
DQ = D // NQ
TILE = 384
AHEAD = 2
YLAG = 2
XT, YT, ZT = 4, 5, 3
PACE = 1


def nt(a, b):
    return lax.dot_general(a, b, (((1,), (1,)), ((), ())), preferred_element_type=F32)


def mm(a, b):
    return jnp.dot(a, b, preferred_element_type=F32)


PQ = 512


def pcols(q):
    return pl.ds(q * PQ, PQ)


def cols(q):
    return pl.ds(q * DQ, DQ)


def kernel(
    attn_in, ow_in, resid_in, gain, ids, wts, wgu_in, wd_in, out,
    attn, ow, resid, in_sem,
    mixed, far, nbr, far_in, nbr_in, meta_out, meta, vrow, gather, comb, gw,
    tok, ysend, yrecv, xrecv, xback, yback, zrecv, wgu, wd, acc, hidden,
    wl_sem, ws_sem, wr_sem, fs_sem, fr_sem, ns_sem, nr_sem, ms_sem, mr_sem,
    as_sem, ar_sem, ys_sem, yr_sem, xs_sem, xr_sem, bs_sem, br_sem, cs_sem, cr_sem, zs_sem, zr_sem,
):
    e = lax.axis_index("expert")
    x = lax.axis_index("tensor")
    z = e // GROUP
    y = (e // NC) % NY
    c = e % NC
    own_d = e % GROUP
    xr, xl = (x + 1) % NX, (x + NX - 1) % NX
    flip = x + 1 - 2 * (x % 2)
    mirror = NX - 1 - x
    wx = (1 - c) * mirror + c * flip
    px = (1 - c) * flip + c * mirror

    def at_z(dz):
        return (((z + dz + NZ) % NZ) * GROUP + own_d, x)

    def at_yc(j):
        return (z * GROUP + ((y + j // NC) % NY) * NC + (c + j % NC) % NC, x)

    def d_from(j):
        return ((y + NY - j // NC) % NY) * NC + (c + j % NC) % NC

    def d_to(j):
        return ((y + j // NC) % NY) * NC + (c + j % NC) % NC

    def rcopy(src, dst, send, recv, dev):
        return pltpu.make_async_remote_copy(
            src_ref=src, dst_ref=dst, send_sem=send, recv_sem=recv, device_id=dev, device_id_type=MESH
        )

    def landed(ref, sem):
        pltpu.make_async_copy(ref, ref, sem).wait()

    inputs = [
        pltpu.make_async_copy(attn_in, attn, in_sem.at[0]),
        pltpu.make_async_copy(ow_in, ow, in_sem.at[1]),
        pltpu.make_async_copy(resid_in, resid, in_sem.at[2]),
    ]
    wloc = [
        pltpu.make_async_copy(wgu_in.at[0], wgu.at[0, pl.ds(0, HID)], wl_sem.at[0]),
        pltpu.make_async_copy(wgu_in.at[1], wgu.at[1, pl.ds(0, HID)], wl_sem.at[1]),
        pltpu.make_async_copy(wd_in, wd.at[pl.ds(0, HID)], wl_sem.at[2]),
    ]
    for copy in inputs + wloc:
        copy.start()

    barrier = pltpu.get_barrier_semaphore()
    peers = [at_z(k) for k in range(1, NZ)] + [at_yc(j) for j in range(1, GROUP)] + [(e, xr), (e, xl)]
    for dev in peers:
        pl.semaphore_signal(barrier, inc=1, device_id=dev, device_id_type=MESH)
    pl.semaphore_wait(barrier, len(peers))

    inputs[0].wait()
    inputs[1].wait()

    def project(owner, q):
        return mm(attn[pl.ds(pl.multiple_of(owner * TOK, TOK), TOK), :], ow[:, pcols(q)])

    opposite = (x + 2) % NX
    far_copy = []
    for side in range(2):
        for q in (2 * side, 2 * side + 1):
            far[side, :, pl.ds((q % 2) * PQ, PQ)] = project(opposite, q).astype(BF16)
        far_copy.append(
            rcopy(far.at[side], far_in.at[side], fs_sem.at[side], fr_sem.at[side], (e, (xr, xl)[side]))
        )
        far_copy[-1].start()
    nbr_copy = []
    for side in range(2):
        part = 1 - side
        for q in (2 * part, 2 * part + 1):
            nbr[side, part, :, pl.ds((q % 2) * PQ, PQ)] = project((xr, xl)[side], q).astype(BF16)
        nbr_copy.append(
            rcopy(nbr.at[side, part], nbr_in.at[side, part], ns_sem.at[side, part], nr_sem.at[side, part], (e, (xr, xl)[side]))
        )
        nbr_copy[-1].start()
    for side in range(2):
        part = side
        for q in (2 * part, 2 * part + 1):
            mixed[:, pcols(q)] = project((xr, xl)[side], q)
        landed(far_in.at[side], fr_sem.at[side])
        for q in (2 * part, 2 * part + 1):
            at = pl.ds((q % 2) * PQ, PQ)
            nbr[side, part, :, at] = (mixed[:, pcols(q)] + far_in[side, :, at].astype(F32)).astype(BF16)
        nbr_copy.append(
            rcopy(nbr.at[side, part], nbr_in.at[side, part], ns_sem.at[side, part], nr_sem.at[side, part], (e, (xr, xl)[side]))
        )
        nbr_copy[-1].start()
    wrem = [
        rcopy(wgu_in.at[0], wgu.at[0, pl.ds(HID, HID)], ws_sem.at[0], wr_sem.at[0], (e, wx)),
        rcopy(wgu_in.at[1], wgu.at[1, pl.ds(HID, HID)], ws_sem.at[1], wr_sem.at[1], (e, wx)),
        rcopy(wd_in, wd.at[pl.ds(HID, HID)], ws_sem.at[2], wr_sem.at[2], (e, wx)),
    ]
    for copy in wrem:
        copy.start()

    inputs[2].wait()
    for q in range(4):
        mixed[:, pcols(q)] = project(x, q) + resid[:, pcols(q)].astype(F32)

    expert = lax.broadcasted_iota(jnp.int32, (NZ * GROUP, TOK), 0)
    holds = jnp.zeros((NZ * GROUP, TOK), F32)
    weight = jnp.zeros((NZ * GROUP, TOK), F32)
    for k in range(ids.shape[0]):
        named = expert == ids[k : k + 1, :]
        holds = holds + jnp.where(named, 1.0, 0.0)
        weight = weight + jnp.where(named, wts[k : k + 1, :], 0.0)
    before = lax.broadcasted_iota(jnp.int32, (TOK, TOK), 0) < lax.broadcasted_iota(jnp.int32, (TOK, TOK), 1)
    rank = mm(holds.astype(BF16), jnp.where(before, 1.0, 0.0).astype(BF16))
    place = jnp.where(holds > 0.5, rank + (z * CAP).astype(F32), -1.0)
    for p in range(NZ):
        meta_out[p, 0:GROUP, :] = place[p * GROUP : (p + 1) * GROUP, :]
        meta_out[p, GROUP : 2 * GROUP, :] = weight[p * GROUP : (p + 1) * GROUP, :]
    meta_copy = []
    for k in range(1, NZ):
        to = (z + k) % NZ
        meta_copy.append(rcopy(meta_out.at[to], meta.at[z], ms_sem.at[k], mr_sem.at[k], at_z(k)))
        meta_copy[-1].start()
    meta[z] = meta_out[z]

    for side in range(2):
        for part in range(2):
            landed(nbr_in.at[side, part], nr_sem.at[side, part])
            for q in (2 * part, 2 * part + 1):
                mixed[:, pcols(q)] = mixed[:, pcols(q)] + nbr_in[side, part, :, pl.ds((q % 2) * PQ, PQ)].astype(F32)

    square = jnp.zeros((TOK, 1), F32)
    for q in range(NQ):
        part = mixed[:, cols(q)]
        square = square + jnp.sum(part * part, axis=1, keepdims=True)
    scale = lax.rsqrt(square * (1.0 / D) + eps_norm)

    def hops(q):
        return (4, 3) if q % 2 == 0 else (3, 4)

    def block(s):
        return pl.ds(pl.multiple_of(s * TOK, TOK), TOK)

    sent = {}

    def ag_send(q, side, k):
        s = (z + NZ - (k - 1)) % NZ if side == 0 else (z + k - 1) % NZ
        ref = tok.at[q, block(s)]
        copy = rcopy(ref, ref, as_sem.at[q, side, k - 1], ar_sem.at[q, side, k - 1], at_z(1 if side == 0 else -1))
        copy.start()
        sent.setdefault(("ag", q), []).append(copy)

    def ag_start(q):
        tok[q, block(z), :] = (mixed[:, cols(q)] * scale * gain[:, cols(q)]).astype(BF16)
        for side in range(2):
            ag_send(q, side, 1)

    def ag_step(q, k):
        for side in range(2):
            if k > hops(q)[side]:
                continue
            s = (z + NZ - k) % NZ if side == 0 else (z + k) % NZ
            landed(tok.at[q, block(s)], ar_sem.at[q, side, k - 1])
            if k < hops(q)[side]:
                ag_send(q, side, k + 1)

    def piece(d):
        return pl.ds(pl.multiple_of(d * PIECE, 32), PIECE)

    def gather_step(q):
        def one(i, _):
            at = pl.ds(pl.multiple_of(i * TILE, TILE), TILE)
            ysend[q, at, :] = mm(gather[at, :], tok[q]).astype(BF16)
            return 0

        lax.fori_loop(0, ROWS // TILE, one, 0)
        for j in range(GROUP - 1, 0, -1):
            copy = rcopy(
                ysend.at[q, piece(d_to(j))], yrecv.at[q, piece(own_d)], ys_sem.at[q, j], yr_sem.at[q, j], at_yc(j)
            )
            copy.start()
            sent.setdefault(("y", q), []).append(copy)
        yrecv[q, piece(own_d), :] = ysend[q, piece(own_d), :]

    def share_step(q):
        for j in range(1, GROUP):
            landed(yrecv.at[q, piece(d_from(j))], yr_sem.at[q, j])
        copy = rcopy(yrecv.at[q], xrecv.at[q], xs_sem.at[q], xr_sem.at[q], (e, px))
        copy.start()
        sent[("x", q)] = [copy]

    def hidden_step(q, who):
        if q == 0 and who == 0:
            for copy in wloc:
                copy.wait()
            for i in range(2):
                landed(wgu.at[i, pl.ds(HID, HID)], wr_sem.at[i])
            landed(wd.at[pl.ds(HID, HID)], wr_sem.at[2])
        if who == 1:
            landed(xrecv.at[q], xr_sem.at[q])
        rows = (yrecv, xrecv)[who]

        def one(i, _):
            at = pl.ds(pl.multiple_of(i * TILE, TILE), TILE)
            to = pl.ds(pl.multiple_of(i * TILE + who * ROWS, TILE), TILE)
            lhs = rows[q, at, :]
            gate = nt(lhs, wgu[0, :, cols(q)])
            up = nt(lhs, wgu[1, :, cols(q)])
            if q > 0:
                gate = gate + acc[0, to, :]
                up = up + acc[1, to, :]
            if q < NQ - 1:
                acc[0, to, :] = gate
                acc[1, to, :] = up
            else:
                hidden[to, :] = (gate / (1.0 + jnp.exp(-gate)) * up).astype(BF16)
            return 0

        lax.fori_loop(0, ROWS // TILE, one, 0)

    def masks():
        for k in range(1, NZ):
            landed(meta.at[(z + NZ - k) % NZ], mr_sem.at[k])
        slot = lax.broadcasted_iota(jnp.int32, (PIECE, TOK), 0).astype(F32)
        eye = jnp.where(
            lax.broadcasted_iota(jnp.int32, (TOK, TOK), 0) == lax.broadcasted_iota(jnp.int32, (TOK, TOK), 1), 1.0, 0.0
        ).astype(BF16)
        for s in range(NZ):
            for d in range(GROUP):
                taken = slot == meta[s, d : d + 1, :]
                gather[d * PIECE : (d + 1) * PIECE, s * TOK : (s + 1) * TOK] = jnp.where(taken, 1.0, 0.0).astype(BF16)
                gw[d * PIECE : (d + 1) * PIECE, :] = jnp.where(
                    taken, meta[s, GROUP + d : GROUP + d + 1, :], 0.0
                ).astype(BF16)
            comb[s * TOK : (s + 1) * TOK, :] = nt(eye, gw[...]).astype(BF16)

    tasks = [(0, 9, masks)]
    for q in range(NQ):
        t = q * PACE
        tasks.append((t, 0, functools.partial(ag_start, q)))
        for k in range(1, 5):
            tasks.append((t + k, 1, functools.partial(ag_step, q, k)))
        tasks.append((t + 4, 2, functools.partial(gather_step, q)))
        tasks.append((t + 4 + YLAG, 3, functools.partial(share_step, q)))
        tasks.append((100 + q, 4, functools.partial(hidden_step, q, 0)))
        tasks.append((200 + q, 5, functools.partial(hidden_step, q, 1)))
    for task in sorted(tasks, key=lambda task: task[:2]):
        task[2]()

    def down_step(q, who):
        for copy in sent[("x", q)]:
            copy.wait_send()
        sent[("x", q)] = []

        def body(i, _):
            at = pl.ds(pl.multiple_of(i * TILE, TILE), TILE)
            of = pl.ds(pl.multiple_of(i * TILE + who * ROWS, TILE), TILE)
            (yrecv, xrecv)[who][q, at, :] = mm(hidden[of, :], wd[:, cols(q)]).astype(BF16)
            return 0

        lax.fori_loop(0, ROWS // TILE, body, 0)
        if who == 1 and q < AHEAD:
            give_back(q)

    def give_back(q):
        if q < NQ:
            copy = rcopy(xrecv.at[q], xback.at[q], bs_sem.at[q], br_sem.at[q], (e, px))
            copy.start()
            sent[("b", q)] = [copy]

    def sum_step(q):
        landed(xback.at[q], br_sem.at[q])
        give_back(q + AHEAD)
        for copy in sent[("y", q)]:
            copy.wait_send()
        ysend[q] = (yrecv[q].astype(F32) + xback[q].astype(F32)).astype(BF16)
        for j in range(GROUP - 1, 0, -1):
            copy = rcopy(
                ysend.at[q, piece(d_to(j))], yback.at[q, piece(own_d)], cs_sem.at[q, j], cr_sem.at[q, j], at_yc(j)
            )
            copy.start()
            sent.setdefault(("c", q), []).append(copy)
        yback[q, piece(own_d), :] = ysend[q, piece(own_d), :]

    def rs_send(q, side, j):
        far_hops = hops(q)[side]
        k = far_hops + 1 - j
        s = (z + k) % NZ if side == 0 else (z + NZ - k) % NZ
        copy = rcopy(
            tok.at[q, block(s)], zrecv.at[q, side, j - 1], zs_sem.at[q, side, j - 1], zr_sem.at[q, side, j - 1],
            at_z(1 if side == 0 else -1),
        )
        copy.start()
        sent.setdefault(("z", q), []).append(copy)

    def combine_step(q):
        for j in range(1, GROUP):
            landed(yback.at[q, piece(d_from(j))], cr_sem.at[q, j])
        for copy in sent[("ag", q)]:
            copy.wait_send()

        def one(i, _):
            at = pl.ds(pl.multiple_of(i * 256, 256), 256)
            tok[q, at, :] = mm(comb[at, :], yback[q]).astype(BF16)
            return 0

        lax.fori_loop(0, NZ * TOK // 256, one, 0)
        for side in range(2):
            rs_send(q, side, 1)

    def rs_step(q, j):
        for side in range(2):
            far_hops = hops(q)[side]
            if j > far_hops:
                continue
            landed(zrecv.at[q, side, j - 1], zr_sem.at[q, side, j - 1])
            if j == far_hops:
                mixed[:, cols(q)] = mixed[:, cols(q)] + zrecv[q, side, j - 1].astype(F32)
                continue
            k = far_hops - j
            s = (z + k) % NZ if side == 0 else (z + NZ - k) % NZ
            tok[q, block(s), :] = (tok[q, block(s), :].astype(F32) + zrecv[q, side, j - 1].astype(F32)).astype(BF16)
            rs_send(q, side, j + 1)

    def finish(q):
        out[:, cols(q)] = (mixed[:, cols(q)] + tok[q, block(z), :].astype(F32)).astype(BF16)

    tasks = []
    for q in range(NQ):
        t = (q + 1) * XT
        tasks.append((-200 + q, 0, functools.partial(down_step, q, 1)))
        tasks.append((-100 + q, 0, functools.partial(down_step, q, 0)))
        tasks.append((t, 1, functools.partial(sum_step, q)))
        tasks.append((t + YT, 2, functools.partial(combine_step, q)))
        for j in range(1, 5):
            tasks.append((t + YT + j * ZT, 3, functools.partial(rs_step, q, j)))
        tasks.append((t + YT + 4 * ZT, 4, functools.partial(finish, q)))
    for task in sorted(tasks, key=lambda task: task[:2]):
        task[2]()

    for copy in far_copy + nbr_copy + meta_copy + wrem:
        copy.wait_send()
    for q in range(NQ):
        for kind in ("b", "c", "z"):
            for copy in sent[(kind, q)]:
                copy.wait_send()


def on_device(
    attn_heads, o_weight, resid, norm_gain, expert_ids, combine_weights, w_gate_up, w_down
):
    vmem = pl.BlockSpec(memory_space=pltpu.VMEM)
    hbm = pl.BlockSpec(memory_space=pl.ANY)
    dma = pltpu.SemaphoreType.DMA
    return pl.pallas_call(
        kernel,
        out_shape=jax.ShapeDtypeStruct((TOK, D), BF16),
        in_specs=[hbm] * 3 + [vmem] * 3 + [hbm] * 2,
        out_specs=vmem,
        scratch_shapes=[
            pltpu.VMEM((4 * TOK, D // NX), BF16),
            pltpu.VMEM((D // NX, D), BF16),
            pltpu.VMEM((TOK, D), BF16),
            dma((3,)),
            pltpu.VMEM((TOK, D), F32),
            pltpu.VMEM((2, TOK, D // 2), BF16),
            pltpu.VMEM((2, 2, TOK, D // 2), BF16),
            pltpu.VMEM((2, TOK, D // 2), BF16),
            pltpu.VMEM((2, 2, TOK, D // 2), BF16),
            pltpu.VMEM((NZ, 2 * GROUP, TOK), F32),
            pltpu.VMEM((NZ, 2 * GROUP, TOK), F32),
            pltpu.VMEM((8, TOK), F32),
            pltpu.VMEM((ROWS, NZ * TOK), BF16),
            pltpu.VMEM((NZ * TOK, ROWS), BF16),
            pltpu.VMEM((ROWS, TOK), BF16),
            pltpu.VMEM((NQ, NZ * TOK, DQ), BF16),
            pltpu.VMEM((NQ, ROWS, DQ), BF16),
            pltpu.VMEM((NQ, ROWS, DQ), BF16),
            pltpu.VMEM((NQ, ROWS, DQ), BF16),
            pltpu.VMEM((NQ, ROWS, DQ), BF16),
            pltpu.VMEM((NQ, ROWS, DQ), BF16),
            pltpu.VMEM((NQ, 2, 4, TOK, DQ), BF16),
            pltpu.VMEM((2, 2 * HID, D), BF16),
            pltpu.VMEM((2 * HID, D), BF16),
            pltpu.VMEM((2, 2 * ROWS, 2 * HID), F32),
            pltpu.VMEM((2 * ROWS, 2 * HID), BF16),
            dma((3,)), dma((3,)), dma((3,)),
            dma((2,)), dma((2,)), dma((2, 2)), dma((2, 2)), dma((NZ,)), dma((NZ,)),
            dma((NQ, 2, 4)), dma((NQ, 2, 4)), dma((NQ, GROUP)), dma((NQ, GROUP)), dma((NQ,)), dma((NQ,)),
            dma((NQ,)), dma((NQ,)), dma((NQ, GROUP)), dma((NQ, GROUP)), dma((NQ, 2, 4)), dma((NQ, 2, 4)),
        ],
        compiler_params=pltpu.CompilerParams(
            collective_id=0, has_side_effects=True, vmem_limit_bytes=60 * 2**20
        ),
        cost_estimate=pl.CostEstimate(flops=16 * 10**9, bytes_accessed=10**7, transcendentals=10**6),
    )(
        attn_heads, o_weight, resid, norm_gain[None, :], expert_ids.T, combine_weights.T,
        jnp.swapaxes(w_gate_up[0], 1, 2), w_down[0],
    )


def solution(mesh):
    in_specs = (
        P("expert", "tensor"),
        P("tensor", None),
        P(("expert", "tensor"), None),
        P(),
        P(("expert", "tensor"), None),
        P(("expert", "tensor"), None),
        P("expert", None, None, "tensor"),
        P("expert", "tensor", None),
    )
    out_specs = P(("expert", "tensor"), None)
    return jax.shard_map(
        on_device, mesh=mesh, in_specs=in_specs, out_specs=out_specs, check_vma=False
    )
```

```python
import functools

import jax
import jax.numpy as jnp
from jax import lax
from jax.experimental import pallas as pl
from jax.experimental.pallas import tpu as pltpu
from jax.sharding import PartitionSpec as P

MESH = pl.DeviceIdType.MESH
BF16 = jnp.bfloat16
F32 = jnp.float32
eps_norm = 1e-06

NZ, NY, NC, NX = 8, 4, 2, 4
GROUP = NY * NC
TOK = 128
D = 2048
CAP = 11
PIECE = 96
ROWS = GROUP * PIECE
HID = 352
NQ = 8
DQ = D // NQ
TILE = 384
YLAG = 2
XT, YT, ZT = 4, 5, 3
THEIR = (0, 0.5, 1, 2, 3, 3.5, 5, 6)
OUR = (1.5, 2.5, 5.5, 6.5, 9, 9.5, 13, 13.5)
PACE = 1


def nt(a, b):
    return lax.dot_general(a, b, (((1,), (1,)), ((), ())), preferred_element_type=F32)


def mm(a, b):
    return jnp.dot(a, b, preferred_element_type=F32)


PQ = 512


def pcols(q):
    return pl.ds(q * PQ, PQ)


def cols(q):
    return pl.ds(q * DQ, DQ)


def kernel(
    attn_in, ow_in, resid_in, gain, ids, wts, wgu_in, wd_in, out,
    attn, ow, resid, in_sem,
    mixed, far, nbr, far_in, nbr_in, meta_out, meta, vrow, gather, comb, gw,
    tok, ysend, yrecv, xrecv, xback, yback, zrecv, wgu, wd, acc, hidden,
    wl_sem, ws_sem, wr_sem, fs_sem, fr_sem, ns_sem, nr_sem, ms_sem, mr_sem,
    as_sem, ar_sem, ys_sem, yr_sem, xs_sem, xr_sem, bs_sem, br_sem, cs_sem, cr_sem, zs_sem, zr_sem,
):
    e = lax.axis_index("expert")
    x = lax.axis_index("tensor")
    z = e // GROUP
    y = (e // NC) % NY
    c = e % NC
    own_d = e % GROUP
    xr, xl = (x + 1) % NX, (x + NX - 1) % NX
    flip = x + 1 - 2 * (x % 2)
    mirror = NX - 1 - x
    wx = (1 - c) * mirror + c * flip
    px = (1 - c) * flip + c * mirror

    def at_z(dz):
        return (((z + dz + NZ) % NZ) * GROUP + own_d, x)

    def at_yc(j):
        return (z * GROUP + ((y + j // NC) % NY) * NC + (c + j % NC) % NC, x)

    def d_from(j):
        return ((y + NY - j // NC) % NY) * NC + (c + j % NC) % NC

    def d_to(j):
        return ((y + j // NC) % NY) * NC + (c + j % NC) % NC

    def rcopy(src, dst, send, recv, dev):
        return pltpu.make_async_remote_copy(
            src_ref=src, dst_ref=dst, send_sem=send, recv_sem=recv, device_id=dev, device_id_type=MESH
        )

    def landed(ref, sem):
        pltpu.make_async_copy(ref, ref, sem).wait()

    inputs = [
        pltpu.make_async_copy(attn_in, attn, in_sem.at[0]),
        pltpu.make_async_copy(ow_in, ow, in_sem.at[1]),
        pltpu.make_async_copy(resid_in, resid, in_sem.at[2]),
    ]
    wloc = [
        pltpu.make_async_copy(wgu_in.at[0], wgu.at[0, pl.ds(0, HID)], wl_sem.at[0]),
        pltpu.make_async_copy(wgu_in.at[1], wgu.at[1, pl.ds(0, HID)], wl_sem.at[1]),
        pltpu.make_async_copy(wd_in, wd.at[pl.ds(0, HID)], wl_sem.at[2]),
    ]
    for copy in inputs + wloc:
        copy.start()

    barrier = pltpu.get_barrier_semaphore()
    peers = [at_z(k) for k in range(1, NZ)] + [at_yc(j) for j in range(1, GROUP)] + [(e, xr), (e, xl)]
    for dev in peers:
        pl.semaphore_signal(barrier, inc=1, device_id=dev, device_id_type=MESH)
    pl.semaphore_wait(barrier, len(peers))

    inputs[0].wait()
    inputs[1].wait()

    def project(owner, q):
        return mm(attn[pl.ds(pl.multiple_of(owner * TOK, TOK), TOK), :], ow[:, pcols(q)])

    opposite = (x + 2) % NX
    far_copy = []
    for side in range(2):
        for q in (2 * side, 2 * side + 1):
            far[side, :, pl.ds((q % 2) * PQ, PQ)] = project(opposite, q).astype(BF16)
        far_copy.append(
            rcopy(far.at[side], far_in.at[side], fs_sem.at[side], fr_sem.at[side], (e, (xr, xl)[side]))
        )
        far_copy[-1].start()
    nbr_copy = []
    for side in range(2):
        part = 1 - side
        for q in (2 * part, 2 * part + 1):
            nbr[side, part, :, pl.ds((q % 2) * PQ, PQ)] = project((xr, xl)[side], q).astype(BF16)
        nbr_copy.append(
            rcopy(nbr.at[side, part], nbr_in.at[side, part], ns_sem.at[side, part], nr_sem.at[side, part], (e, (xr, xl)[side]))
        )
        nbr_copy[-1].start()
    for side in range(2):
        part = side
        for q in (2 * part, 2 * part + 1):
            mixed[:, pcols(q)] = project((xr, xl)[side], q)
        landed(far_in.at[side], fr_sem.at[side])
        for q in (2 * part, 2 * part + 1):
            at = pl.ds((q % 2) * PQ, PQ)
            nbr[side, part, :, at] = (mixed[:, pcols(q)] + far_in[side, :, at].astype(F32)).astype(BF16)
        nbr_copy.append(
            rcopy(nbr.at[side, part], nbr_in.at[side, part], ns_sem.at[side, part], nr_sem.at[side, part], (e, (xr, xl)[side]))
        )
        nbr_copy[-1].start()
    wrem = [
        rcopy(wgu_in.at[0], wgu.at[0, pl.ds(HID, HID)], ws_sem.at[0], wr_sem.at[0], (e, wx)),
        rcopy(wgu_in.at[1], wgu.at[1, pl.ds(HID, HID)], ws_sem.at[1], wr_sem.at[1], (e, wx)),
        rcopy(wd_in, wd.at[pl.ds(HID, HID)], ws_sem.at[2], wr_sem.at[2], (e, wx)),
    ]
    for copy in wrem:
        copy.start()

    inputs[2].wait()
    for q in range(4):
        mixed[:, pcols(q)] = project(x, q) + resid[:, pcols(q)].astype(F32)

    expert = lax.broadcasted_iota(jnp.int32, (NZ * GROUP, TOK), 0)
    holds = jnp.zeros((NZ * GROUP, TOK), F32)
    weight = jnp.zeros((NZ * GROUP, TOK), F32)
    for k in range(ids.shape[0]):
        named = expert == ids[k : k + 1, :]
        holds = holds + jnp.where(named, 1.0, 0.0)
        weight = weight + jnp.where(named, wts[k : k + 1, :], 0.0)
    before = lax.broadcasted_iota(jnp.int32, (TOK, TOK), 0) < lax.broadcasted_iota(jnp.int32, (TOK, TOK), 1)
    rank = mm(holds.astype(BF16), jnp.where(before, 1.0, 0.0).astype(BF16))
    place = jnp.where(holds > 0.5, rank + (z * CAP).astype(F32), -1.0)
    for p in range(NZ):
        meta_out[p, 0:GROUP, :] = place[p * GROUP : (p + 1) * GROUP, :]
        meta_out[p, GROUP : 2 * GROUP, :] = weight[p * GROUP : (p + 1) * GROUP, :]
    meta_copy = []
    for k in range(1, NZ):
        to = (z + k) % NZ
        meta_copy.append(rcopy(meta_out.at[to], meta.at[z], ms_sem.at[k], mr_sem.at[k], at_z(k)))
        meta_copy[-1].start()
    meta[z] = meta_out[z]

    for side in range(2):
        for part in range(2):
            landed(nbr_in.at[side, part], nr_sem.at[side, part])
            for q in (2 * part, 2 * part + 1):
                mixed[:, pcols(q)] = mixed[:, pcols(q)] + nbr_in[side, part, :, pl.ds((q % 2) * PQ, PQ)].astype(F32)

    square = jnp.zeros((TOK, 1), F32)
    for q in range(NQ):
        part = mixed[:, cols(q)]
        square = square + jnp.sum(part * part, axis=1, keepdims=True)
    scale = lax.rsqrt(square * (1.0 / D) + eps_norm)

    def hops(q):
        return (4, 3) if q % 2 == 0 else (3, 4)

    def block(s):
        return pl.ds(pl.multiple_of(s * TOK, TOK), TOK)

    sent = {}

    def ag_send(q, side, k):
        s = (z + NZ - (k - 1)) % NZ if side == 0 else (z + k - 1) % NZ
        ref = tok.at[q, block(s)]
        copy = rcopy(ref, ref, as_sem.at[q, side, k - 1], ar_sem.at[q, side, k - 1], at_z(1 if side == 0 else -1))
        copy.start()
        sent.setdefault(("ag", q), []).append(copy)

    def ag_start(q):
        tok[q, block(z), :] = (mixed[:, cols(q)] * scale * gain[:, cols(q)]).astype(BF16)
        for side in range(2):
            ag_send(q, side, 1)

    def ag_step(q, k):
        for side in range(2):
            if k > hops(q)[side]:
                continue
            s = (z + NZ - k) % NZ if side == 0 else (z + k) % NZ
            landed(tok.at[q, block(s)], ar_sem.at[q, side, k - 1])
            if k < hops(q)[side]:
                ag_send(q, side, k + 1)

    def piece(d):
        return pl.ds(pl.multiple_of(d * PIECE, 32), PIECE)

    def gather_step(q):
        def one(i, _):
            at = pl.ds(pl.multiple_of(i * TILE, TILE), TILE)
            ysend[q, at, :] = mm(gather[at, :], tok[q]).astype(BF16)
            return 0

        lax.fori_loop(0, ROWS // TILE, one, 0)
        for j in range(GROUP - 1, 0, -1):
            copy = rcopy(
                ysend.at[q, piece(d_to(j))], yrecv.at[q, piece(own_d)], ys_sem.at[q, j], yr_sem.at[q, j], at_yc(j)
            )
            copy.start()
            sent.setdefault(("y", q), []).append(copy)
        yrecv[q, piece(own_d), :] = ysend[q, piece(own_d), :]

    def share_step(q):
        for j in range(1, GROUP):
            landed(yrecv.at[q, piece(d_from(j))], yr_sem.at[q, j])
        copy = rcopy(yrecv.at[q], xrecv.at[q], xs_sem.at[q], xr_sem.at[q], (e, px))
        copy.start()
        sent[("x", q)] = [copy]

    def hidden_step(q, who):
        if q == 0 and who == 0:
            for copy in wloc:
                copy.wait()
            for i in range(2):
                landed(wgu.at[i, pl.ds(HID, HID)], wr_sem.at[i])
            landed(wd.at[pl.ds(HID, HID)], wr_sem.at[2])
        if who == 1:
            landed(xrecv.at[q], xr_sem.at[q])
        rows = (yrecv, xrecv)[who]

        def one(i, _):
            at = pl.ds(pl.multiple_of(i * TILE, TILE), TILE)
            to = pl.ds(pl.multiple_of(i * TILE + who * ROWS, TILE), TILE)
            lhs = rows[q, at, :]
            gate = nt(lhs, wgu[0, :, cols(q)])
            up = nt(lhs, wgu[1, :, cols(q)])
            if q > 0:
                gate = gate + acc[0, to, :]
                up = up + acc[1, to, :]
            if q < NQ - 1:
                acc[0, to, :] = gate
                acc[1, to, :] = up
            else:
                hidden[to, :] = (gate / (1.0 + jnp.exp(-gate)) * up).astype(BF16)
            return 0

        lax.fori_loop(0, ROWS // TILE, one, 0)

    def masks():
        for k in range(1, NZ):
            landed(meta.at[(z + NZ - k) % NZ], mr_sem.at[k])
        slot = lax.broadcasted_iota(jnp.int32, (PIECE, TOK), 0).astype(F32)
        eye = jnp.where(
            lax.broadcasted_iota(jnp.int32, (TOK, TOK), 0) == lax.broadcasted_iota(jnp.int32, (TOK, TOK), 1), 1.0, 0.0
        ).astype(BF16)
        for s in range(NZ):
            for d in range(GROUP):
                taken = slot == meta[s, d : d + 1, :]
                gather[d * PIECE : (d + 1) * PIECE, s * TOK : (s + 1) * TOK] = jnp.where(taken, 1.0, 0.0).astype(BF16)
                gw[d * PIECE : (d + 1) * PIECE, :] = jnp.where(
                    taken, meta[s, GROUP + d : GROUP + d + 1, :], 0.0
                ).astype(BF16)
            comb[s * TOK : (s + 1) * TOK, :] = nt(eye, gw[...]).astype(BF16)

    tasks = [(0, 9, masks)]
    for q in range(NQ):
        t = q * PACE
        tasks.append((t, 0, functools.partial(ag_start, q)))
        for k in range(1, 5):
            tasks.append((t + k, 1, functools.partial(ag_step, q, k)))
        tasks.append((t + 4, 2, functools.partial(gather_step, q)))
        tasks.append((t + 4 + YLAG, 3, functools.partial(share_step, q)))
        tasks.append((100 + q, 4, functools.partial(hidden_step, q, 0)))
        tasks.append((200 + q, 5, functools.partial(hidden_step, q, 1)))
    for task in sorted(tasks, key=lambda task: task[:2]):
        task[2]()

    def down_step(q, who):
        for copy in sent[("x", q)]:
            copy.wait_send()
        sent[("x", q)] = []

        def body(i, _):
            at = pl.ds(pl.multiple_of(i * TILE, TILE), TILE)
            of = pl.ds(pl.multiple_of(i * TILE + who * ROWS, TILE), TILE)
            (yrecv, xrecv)[who][q, at, :] = mm(hidden[of, :], wd[:, cols(q)]).astype(BF16)
            return 0

        lax.fori_loop(0, ROWS // TILE, body, 0)
        if who == 1:
            copy = rcopy(xrecv.at[q], xback.at[q], bs_sem.at[q], br_sem.at[q], (e, px))
            copy.start()
            sent[("b", q)] = [copy]

    def sum_step(q):
        landed(xback.at[q], br_sem.at[q])
        for copy in sent[("y", q)]:
            copy.wait_send()
        ysend[q] = (yrecv[q].astype(F32) + xback[q].astype(F32)).astype(BF16)
        for j in range(GROUP - 1, 0, -1):
            copy = rcopy(
                ysend.at[q, piece(d_to(j))], yback.at[q, piece(own_d)], cs_sem.at[q, j], cr_sem.at[q, j], at_yc(j)
            )
            copy.start()
            sent.setdefault(("c", q), []).append(copy)
        yback[q, piece(own_d), :] = ysend[q, piece(own_d), :]

    def rs_send(q, side, j):
        far_hops = hops(q)[side]
        k = far_hops + 1 - j
        s = (z + k) % NZ if side == 0 else (z + NZ - k) % NZ
        copy = rcopy(
            tok.at[q, block(s)], zrecv.at[q, side, j - 1], zs_sem.at[q, side, j - 1], zr_sem.at[q, side, j - 1],
            at_z(1 if side == 0 else -1),
        )
        copy.start()
        sent.setdefault(("z", q), []).append(copy)

    def combine_step(q):
        for j in range(1, GROUP):
            landed(yback.at[q, piece(d_from(j))], cr_sem.at[q, j])
        for copy in sent[("ag", q)]:
            copy.wait_send()

        def one(i, _):
            at = pl.ds(pl.multiple_of(i * 256, 256), 256)
            tok[q, at, :] = mm(comb[at, :], yback[q]).astype(BF16)
            return 0

        lax.fori_loop(0, NZ * TOK // 256, one, 0)
        for side in range(2):
            rs_send(q, side, 1)

    def rs_step(q, j):
        for side in range(2):
            far_hops = hops(q)[side]
            if j > far_hops:
                continue
            landed(zrecv.at[q, side, j - 1], zr_sem.at[q, side, j - 1])
            if j == far_hops:
                mixed[:, cols(q)] = mixed[:, cols(q)] + zrecv[q, side, j - 1].astype(F32)
                continue
            k = far_hops - j
            s = (z + k) % NZ if side == 0 else (z + NZ - k) % NZ
            tok[q, block(s), :] = (tok[q, block(s), :].astype(F32) + zrecv[q, side, j - 1].astype(F32)).astype(BF16)
            rs_send(q, side, j + 1)

    def finish(q):
        out[:, cols(q)] = (mixed[:, cols(q)] + tok[q, block(z), :].astype(F32)).astype(BF16)

    tasks = []
    for q in range(NQ):
        t = (q + 1) * XT
        tasks.append((OUR[q], 0, functools.partial(down_step, q, 0)))
        tasks.append((THEIR[q], 0, functools.partial(down_step, q, 1)))
        tasks.append((t, 1, functools.partial(sum_step, q)))
        tasks.append((t + YT, 2, functools.partial(combine_step, q)))
        for j in range(1, 5):
            tasks.append((t + YT + j * ZT, 3, functools.partial(rs_step, q, j)))
        tasks.append((t + YT + 4 * ZT, 4, functools.partial(finish, q)))
    for task in sorted(tasks, key=lambda task: task[:2]):
        task[2]()

    for copy in far_copy + nbr_copy + meta_copy + wrem:
        copy.wait_send()
    for q in range(NQ):
        for kind in ("b", "c", "z"):
            for copy in sent[(kind, q)]:
                copy.wait_send()


def on_device(
    attn_heads, o_weight, resid, norm_gain, expert_ids, combine_weights, w_gate_up, w_down
):
    vmem = pl.BlockSpec(memory_space=pltpu.VMEM)
    hbm = pl.BlockSpec(memory_space=pl.ANY)
    dma = pltpu.SemaphoreType.DMA
    return pl.pallas_call(
        kernel,
        out_shape=jax.ShapeDtypeStruct((TOK, D), BF16),
        in_specs=[hbm] * 3 + [vmem] * 3 + [hbm] * 2,
        out_specs=vmem,
        scratch_shapes=[
            pltpu.VMEM((4 * TOK, D // NX), BF16),
            pltpu.VMEM((D // NX, D), BF16),
            pltpu.VMEM((TOK, D), BF16),
            dma((3,)),
            pltpu.VMEM((TOK, D), F32),
            pltpu.VMEM((2, TOK, D // 2), BF16),
            pltpu.VMEM((2, 2, TOK, D // 2), BF16),
            pltpu.VMEM((2, TOK, D // 2), BF16),
            pltpu.VMEM((2, 2, TOK, D // 2), BF16),
            pltpu.VMEM((NZ, 2 * GROUP, TOK), F32),
            pltpu.VMEM((NZ, 2 * GROUP, TOK), F32),
            pltpu.VMEM((8, TOK), F32),
            pltpu.VMEM((ROWS, NZ * TOK), BF16),
            pltpu.VMEM((NZ * TOK, ROWS), BF16),
            pltpu.VMEM((ROWS, TOK), BF16),
            pltpu.VMEM((NQ, NZ * TOK, DQ), BF16),
            pltpu.VMEM((NQ, ROWS, DQ), BF16),
            pltpu.VMEM((NQ, ROWS, DQ), BF16),
            pltpu.VMEM((NQ, ROWS, DQ), BF16),
            pltpu.VMEM((NQ, ROWS, DQ), BF16),
            pltpu.VMEM((NQ, ROWS, DQ), BF16),
            pltpu.VMEM((NQ, 2, 4, TOK, DQ), BF16),
            pltpu.VMEM((2, 2 * HID, D), BF16),
            pltpu.VMEM((2 * HID, D), BF16),
            pltpu.VMEM((2, 2 * ROWS, 2 * HID), F32),
            pltpu.VMEM((2 * ROWS, 2 * HID), BF16),
            dma((3,)), dma((3,)), dma((3,)),
            dma((2,)), dma((2,)), dma((2, 2)), dma((2, 2)), dma((NZ,)), dma((NZ,)),
            dma((NQ, 2, 4)), dma((NQ, 2, 4)), dma((NQ, GROUP)), dma((NQ, GROUP)), dma((NQ,)), dma((NQ,)),
            dma((NQ,)), dma((NQ,)), dma((NQ, GROUP)), dma((NQ, GROUP)), dma((NQ, 2, 4)), dma((NQ, 2, 4)),
        ],
        compiler_params=pltpu.CompilerParams(
            collective_id=0, has_side_effects=True, vmem_limit_bytes=60 * 2**20
        ),
        cost_estimate=pl.CostEstimate(flops=16 * 10**9, bytes_accessed=10**7, transcendentals=10**6),
    )(
        attn_heads, o_weight, resid, norm_gain[None, :], expert_ids.T, combine_weights.T,
        jnp.swapaxes(w_gate_up[0], 1, 2), w_down[0],
    )


def solution(mesh):
    in_specs = (
        P("expert", "tensor"),
        P("tensor", None),
        P(("expert", "tensor"), None),
        P(),
        P(("expert", "tensor"), None),
        P(("expert", "tensor"), None),
        P("expert", None, None, "tensor"),
        P("expert", "tensor", None),
    )
    out_specs = P(("expert", "tensor"), None)
    return jax.shard_map(
        on_device, mesh=mesh, in_specs=in_specs, out_specs=out_specs, check_vma=False
    )
```

```python
import functools

import jax
import jax.numpy as jnp
from jax import lax
from jax.experimental import pallas as pl
from jax.experimental.pallas import tpu as pltpu
from jax.sharding import PartitionSpec as P

MESH = pl.DeviceIdType.MESH
BF16 = jnp.bfloat16
F32 = jnp.float32
eps_norm = 1e-06

NZ, NY, NC, NX = 8, 4, 2, 4
GROUP = NY * NC
TOK = 128
D = 2048
CAP = 11
PIECE = 96
ROWS = GROUP * PIECE
HID = 352
NQ = 8
DQ = D // NQ
TILE = 384
YLAG = 2
XT, YT, ZT, ZQ = 4.6, 7, 3.5, 5.5
THEIR = (0, 0.5, 1, 2, 3, 3.5, 5, 6)
OUR = (1.5, 2.5, 5.5, 6.5, 9, 9.5, 13, 13.5)
PACE = 1


def nt(a, b):
    return lax.dot_general(a, b, (((1,), (1,)), ((), ())), preferred_element_type=F32)


def mm(a, b):
    return jnp.dot(a, b, preferred_element_type=F32)


PQ = 512


def pcols(q):
    return pl.ds(q * PQ, PQ)


def cols(q):
    return pl.ds(q * DQ, DQ)


def kernel(
    attn_in, ow_in, resid_in, gain, ids, wts, wgu_in, wd_in, out,
    attn, ow, resid, in_sem,
    mixed, far, nbr, far_in, nbr_in, meta_out, meta, vrow, gather, comb, gw,
    tok, ysend, yrecv, xrecv, xback, yback, zrecv, wgu, wd, acc, hidden,
    wl_sem, ws_sem, wr_sem, fs_sem, fr_sem, ns_sem, nr_sem, ms_sem, mr_sem,
    as_sem, ar_sem, ys_sem, yr_sem, xs_sem, xr_sem, bs_sem, br_sem, cs_sem, cr_sem, zs_sem, zr_sem,
):
    e = lax.axis_index("expert")
    x = lax.axis_index("tensor")
    z = e // GROUP
    y = (e // NC) % NY
    c = e % NC
    own_d = e % GROUP
    xr, xl = (x + 1) % NX, (x + NX - 1) % NX
    flip = x + 1 - 2 * (x % 2)
    mirror = NX - 1 - x
    wx = (1 - c) * mirror + c * flip
    px = (1 - c) * flip + c * mirror

    def at_z(dz):
        return (((z + dz + NZ) % NZ) * GROUP + own_d, x)

    def at_yc(j):
        return (z * GROUP + ((y + j // NC) % NY) * NC + (c + j % NC) % NC, x)

    def d_from(j):
        return ((y + NY - j // NC) % NY) * NC + (c + j % NC) % NC

    def d_to(j):
        return ((y + j // NC) % NY) * NC + (c + j % NC) % NC

    def rcopy(src, dst, send, recv, dev):
        return pltpu.make_async_remote_copy(
            src_ref=src, dst_ref=dst, send_sem=send, recv_sem=recv, device_id=dev, device_id_type=MESH
        )

    def landed(ref, sem):
        pltpu.make_async_copy(ref, ref, sem).wait()

    inputs = [
        pltpu.make_async_copy(attn_in, attn, in_sem.at[0]),
        pltpu.make_async_copy(ow_in, ow, in_sem.at[1]),
        pltpu.make_async_copy(resid_in, resid, in_sem.at[2]),
    ]
    wloc = [
        pltpu.make_async_copy(wgu_in.at[0], wgu.at[0, pl.ds(0, HID)], wl_sem.at[0]),
        pltpu.make_async_copy(wgu_in.at[1], wgu.at[1, pl.ds(0, HID)], wl_sem.at[1]),
        pltpu.make_async_copy(wd_in, wd.at[pl.ds(0, HID)], wl_sem.at[2]),
    ]
    for copy in inputs + wloc:
        copy.start()

    barrier = pltpu.get_barrier_semaphore()
    peers = [at_z(k) for k in range(1, NZ)] + [at_yc(j) for j in range(1, GROUP)] + [(e, xr), (e, xl)]
    for dev in peers:
        pl.semaphore_signal(barrier, inc=1, device_id=dev, device_id_type=MESH)
    pl.semaphore_wait(barrier, len(peers))

    inputs[0].wait()
    inputs[1].wait()

    def project(owner, q):
        return mm(attn[pl.ds(pl.multiple_of(owner * TOK, TOK), TOK), :], ow[:, pcols(q)])

    opposite = (x + 2) % NX
    far_copy = []
    for side in range(2):
        for q in (2 * side, 2 * side + 1):
            far[side, :, pl.ds((q % 2) * PQ, PQ)] = project(opposite, q).astype(BF16)
        far_copy.append(
            rcopy(far.at[side], far_in.at[side], fs_sem.at[side], fr_sem.at[side], (e, (xr, xl)[side]))
        )
        far_copy[-1].start()
    nbr_copy = []
    for side in range(2):
        part = 1 - side
        for q in (2 * part, 2 * part + 1):
            nbr[side, part, :, pl.ds((q % 2) * PQ, PQ)] = project((xr, xl)[side], q).astype(BF16)
        nbr_copy.append(
            rcopy(nbr.at[side, part], nbr_in.at[side, part], ns_sem.at[side, part], nr_sem.at[side, part], (e, (xr, xl)[side]))
        )
        nbr_copy[-1].start()
    for side in range(2):
        part = side
        for q in (2 * part, 2 * part + 1):
            mixed[:, pcols(q)] = project((xr, xl)[side], q)
        landed(far_in.at[side], fr_sem.at[side])
        for q in (2 * part, 2 * part + 1):
            at = pl.ds((q % 2) * PQ, PQ)
            nbr[side, part, :, at] = (mixed[:, pcols(q)] + far_in[side, :, at].astype(F32)).astype(BF16)
        nbr_copy.append(
            rcopy(nbr.at[side, part], nbr_in.at[side, part], ns_sem.at[side, part], nr_sem.at[side, part], (e, (xr, xl)[side]))
        )
        nbr_copy[-1].start()
    wrem = [
        rcopy(wgu_in.at[0], wgu.at[0, pl.ds(HID, HID)], ws_sem.at[0], wr_sem.at[0], (e, wx)),
        rcopy(wgu_in.at[1], wgu.at[1, pl.ds(HID, HID)], ws_sem.at[1], wr_sem.at[1], (e, wx)),
        rcopy(wd_in, wd.at[pl.ds(HID, HID)], ws_sem.at[2], wr_sem.at[2], (e, wx)),
    ]
    for copy in wrem:
        copy.start()

    inputs[2].wait()
    for q in range(4):
        mixed[:, pcols(q)] = project(x, q) + resid[:, pcols(q)].astype(F32)

    expert = lax.broadcasted_iota(jnp.int32, (NZ * GROUP, TOK), 0)
    holds = jnp.zeros((NZ * GROUP, TOK), F32)
    weight = jnp.zeros((NZ * GROUP, TOK), F32)
    for k in range(ids.shape[0]):
        named = expert == ids[k : k + 1, :]
        holds = holds + jnp.where(named, 1.0, 0.0)
        weight = weight + jnp.where(named, wts[k : k + 1, :], 0.0)
    before = lax.broadcasted_iota(jnp.int32, (TOK, TOK), 0) < lax.broadcasted_iota(jnp.int32, (TOK, TOK), 1)
    rank = mm(holds.astype(BF16), jnp.where(before, 1.0, 0.0).astype(BF16))
    place = jnp.where(holds > 0.5, rank + (z * CAP).astype(F32), -1.0)
    for p in range(NZ):
        meta_out[p, 0:GROUP, :] = place[p * GROUP : (p + 1) * GROUP, :]
        meta_out[p, GROUP : 2 * GROUP, :] = weight[p * GROUP : (p + 1) * GROUP, :]
    meta_copy = []
    for k in range(1, NZ):
        to = (z + k) % NZ
        meta_copy.append(rcopy(meta_out.at[to], meta.at[z], ms_sem.at[k], mr_sem.at[k], at_z(k)))
        meta_copy[-1].start()
    meta[z] = meta_out[z]

    for side in range(2):
        for part in range(2):
            landed(nbr_in.at[side, part], nr_sem.at[side, part])
            for q in (2 * part, 2 * part + 1):
                mixed[:, pcols(q)] = mixed[:, pcols(q)] + nbr_in[side, part, :, pl.ds((q % 2) * PQ, PQ)].astype(F32)

    square = jnp.zeros((TOK, 1), F32)
    for q in range(NQ):
        part = mixed[:, cols(q)]
        square = square + jnp.sum(part * part, axis=1, keepdims=True)
    scale = lax.rsqrt(square * (1.0 / D) + eps_norm)

    def hops(q):
        return (4, 3) if q % 2 == 0 else (3, 4)

    def block(s):
        return pl.ds(pl.multiple_of(s * TOK, TOK), TOK)

    sent = {}

    def ag_send(q, side, k):
        s = (z + NZ - (k - 1)) % NZ if side == 0 else (z + k - 1) % NZ
        ref = tok.at[q, block(s)]
        copy = rcopy(ref, ref, as_sem.at[q, side, k - 1], ar_sem.at[q, side, k - 1], at_z(1 if side == 0 else -1))
        copy.start()
        sent.setdefault(("ag", q), []).append(copy)

    def ag_start(q):
        tok[q, block(z), :] = (mixed[:, cols(q)] * scale * gain[:, cols(q)]).astype(BF16)
        for side in range(2):
            ag_send(q, side, 1)

    def ag_step(q, k):
        for side in range(2):
            if k > hops(q)[side]:
                continue
            s = (z + NZ - k) % NZ if side == 0 else (z + k) % NZ
            landed(tok.at[q, block(s)], ar_sem.at[q, side, k - 1])
            if k < hops(q)[side]:
                ag_send(q, side, k + 1)

    def piece(d):
        return pl.ds(pl.multiple_of(d * PIECE, 32), PIECE)

    def gather_step(q):
        def one(i, _):
            at = pl.ds(pl.multiple_of(i * TILE, TILE), TILE)
            ysend[q, at, :] = mm(gather[at, :], tok[q]).astype(BF16)
            return 0

        lax.fori_loop(0, ROWS // TILE, one, 0)
        for j in range(GROUP - 1, 0, -1):
            copy = rcopy(
                ysend.at[q, piece(d_to(j))], yrecv.at[q, piece(own_d)], ys_sem.at[q, j], yr_sem.at[q, j], at_yc(j)
            )
            copy.start()
            sent.setdefault(("y", q), []).append(copy)
        yrecv[q, piece(own_d), :] = ysend[q, piece(own_d), :]

    def share_step(q):
        for j in range(1, GROUP):
            landed(yrecv.at[q, piece(d_from(j))], yr_sem.at[q, j])
        copy = rcopy(yrecv.at[q], xrecv.at[q], xs_sem.at[q], xr_sem.at[q], (e, px))
        copy.start()
        sent[("x", q)] = [copy]

    def hidden_step(q, who):
        if q == 0 and who == 0:
            for copy in wloc:
                copy.wait()
            for i in range(2):
                landed(wgu.at[i, pl.ds(HID, HID)], wr_sem.at[i])
            landed(wd.at[pl.ds(HID, HID)], wr_sem.at[2])
        if who == 1:
            landed(xrecv.at[q], xr_sem.at[q])
        rows = (yrecv, xrecv)[who]

        def one(i, _):
            at = pl.ds(pl.multiple_of(i * TILE, TILE), TILE)
            to = pl.ds(pl.multiple_of(i * TILE + who * ROWS, TILE), TILE)
            lhs = rows[q, at, :]
            gate = nt(lhs, wgu[0, :, cols(q)])
            up = nt(lhs, wgu[1, :, cols(q)])
            if q > 0:
                gate = gate + acc[0, to, :]
                up = up + acc[1, to, :]
            if q < NQ - 1:
                acc[0, to, :] = gate
                acc[1, to, :] = up
            else:
                hidden[to, :] = (gate / (1.0 + jnp.exp(-gate)) * up).astype(BF16)
            return 0

        lax.fori_loop(0, ROWS // TILE, one, 0)

    def masks():
        for k in range(1, NZ):
            landed(meta.at[(z + NZ - k) % NZ], mr_sem.at[k])
        slot = lax.broadcasted_iota(jnp.int32, (PIECE, TOK), 0).astype(F32)
        eye = jnp.where(
            lax.broadcasted_iota(jnp.int32, (TOK, TOK), 0) == lax.broadcasted_iota(jnp.int32, (TOK, TOK), 1), 1.0, 0.0
        ).astype(BF16)
        for s in range(NZ):
            for d in range(GROUP):
                taken = slot == meta[s, d : d + 1, :]
                gather[d * PIECE : (d + 1) * PIECE, s * TOK : (s + 1) * TOK] = jnp.where(taken, 1.0, 0.0).astype(BF16)
                gw[d * PIECE : (d + 1) * PIECE, :] = jnp.where(
                    taken, meta[s, GROUP + d : GROUP + d + 1, :], 0.0
                ).astype(BF16)
            comb[s * TOK : (s + 1) * TOK, :] = nt(eye, gw[...]).astype(BF16)

    tasks = [(0, 9, masks)]
    for q in range(NQ):
        t = q * PACE
        tasks.append((t, 0, functools.partial(ag_start, q)))
        for k in range(1, 5):
            tasks.append((t + k, 1, functools.partial(ag_step, q, k)))
        tasks.append((t + 4, 2, functools.partial(gather_step, q)))
        tasks.append((t + 4 + YLAG, 3, functools.partial(share_step, q)))
        tasks.append((PACE * (NQ + 3) + 0.5 if q < 3 else 100 + q, 4 + q / NQ, functools.partial(hidden_step, q, 0)))
        tasks.append((200 + q, 6, functools.partial(hidden_step, q, 1)))
    for task in sorted(tasks, key=lambda task: task[:2]):
        task[2]()

    def down_step(q, who):
        for copy in sent[("x", q)]:
            copy.wait_send()
        sent[("x", q)] = []

        def body(i, _):
            at = pl.ds(pl.multiple_of(i * TILE, TILE), TILE)
            of = pl.ds(pl.multiple_of(i * TILE + who * ROWS, TILE), TILE)
            (yrecv, xrecv)[who][q, at, :] = mm(hidden[of, :], wd[:, cols(q)]).astype(BF16)
            return 0

        lax.fori_loop(0, ROWS // TILE, body, 0)
        if who == 1:
            copy = rcopy(xrecv.at[q], xback.at[q], bs_sem.at[q], br_sem.at[q], (e, px))
            copy.start()
            sent[("b", q)] = [copy]

    def sum_step(q):
        landed(xback.at[q], br_sem.at[q])
        for copy in sent[("y", q)]:
            copy.wait_send()
        ysend[q] = (yrecv[q].astype(F32) + xback[q].astype(F32)).astype(BF16)
        for j in range(GROUP - 1, 0, -1):
            copy = rcopy(
                ysend.at[q, piece(d_to(j))], yback.at[q, piece(own_d)], cs_sem.at[q, j], cr_sem.at[q, j], at_yc(j)
            )
            copy.start()
            sent.setdefault(("c", q), []).append(copy)
        yback[q, piece(own_d), :] = ysend[q, piece(own_d), :]

    def rs_send(q, side, j):
        far_hops = hops(q)[side]
        k = far_hops + 1 - j
        s = (z + k) % NZ if side == 0 else (z + NZ - k) % NZ
        copy = rcopy(
            tok.at[q, block(s)], zrecv.at[q, side, j - 1], zs_sem.at[q, side, j - 1], zr_sem.at[q, side, j - 1],
            at_z(1 if side == 0 else -1),
        )
        copy.start()
        sent.setdefault(("z", q), []).append(copy)

    def combine_step(q):
        for j in range(1, GROUP):
            landed(yback.at[q, piece(d_from(j))], cr_sem.at[q, j])
        for copy in sent[("ag", q)]:
            copy.wait_send()

        def one(i, _):
            at = pl.ds(pl.multiple_of(i * 256, 256), 256)
            tok[q, at, :] = mm(comb[at, :], yback[q]).astype(BF16)
            return 0

        lax.fori_loop(0, NZ * TOK // 256, one, 0)
        for side in range(2):
            rs_send(q, side, 1)

    def rs_step(q, j):
        for side in range(2):
            far_hops = hops(q)[side]
            if j > far_hops:
                continue
            landed(zrecv.at[q, side, j - 1], zr_sem.at[q, side, j - 1])
            if j == far_hops:
                mixed[:, cols(q)] = mixed[:, cols(q)] + zrecv[q, side, j - 1].astype(F32)
                continue
            k = far_hops - j
            s = (z + k) % NZ if side == 0 else (z + NZ - k) % NZ
            tok[q, block(s), :] = (tok[q, block(s), :].astype(F32) + zrecv[q, side, j - 1].astype(F32)).astype(BF16)
            rs_send(q, side, j + 1)

    def finish(q):
        out[:, cols(q)] = (mixed[:, cols(q)] + tok[q, block(z), :].astype(F32)).astype(BF16)

    tasks = []
    for q in range(NQ):
        t = (q + 1) * XT
        tasks.append((OUR[q], 0, functools.partial(down_step, q, 0)))
        tasks.append((THEIR[q], 0, functools.partial(down_step, q, 1)))
        tasks.append((t, 1, functools.partial(sum_step, q)))
        tasks.append((t + YT, 2, functools.partial(combine_step, q)))
        for j in range(1, 5):
            tasks.append((XT + YT + q * ZQ + j * ZT, 3, functools.partial(rs_step, q, j)))
        tasks.append((XT + YT + q * ZQ + 4 * ZT, 4, functools.partial(finish, q)))
    for task in sorted(tasks, key=lambda task: task[:2]):
        task[2]()

    for copy in far_copy + nbr_copy + meta_copy + wrem:
        copy.wait_send()
    for q in range(NQ):
        for kind in ("b", "c", "z"):
            for copy in sent[(kind, q)]:
                copy.wait_send()


def on_device(
    attn_heads, o_weight, resid, norm_gain, expert_ids, combine_weights, w_gate_up, w_down
):
    vmem = pl.BlockSpec(memory_space=pltpu.VMEM)
    hbm = pl.BlockSpec(memory_space=pl.ANY)
    dma = pltpu.SemaphoreType.DMA
    return pl.pallas_call(
        kernel,
        out_shape=jax.ShapeDtypeStruct((TOK, D), BF16),
        in_specs=[hbm] * 3 + [vmem] * 3 + [hbm] * 2,
        out_specs=vmem,
        scratch_shapes=[
            pltpu.VMEM((4 * TOK, D // NX), BF16),
            pltpu.VMEM((D // NX, D), BF16),
            pltpu.VMEM((TOK, D), BF16),
            dma((3,)),
            pltpu.VMEM((TOK, D), F32),
            pltpu.VMEM((2, TOK, D // 2), BF16),
            pltpu.VMEM((2, 2, TOK, D // 2), BF16),
            pltpu.VMEM((2, TOK, D // 2), BF16),
            pltpu.VMEM((2, 2, TOK, D // 2), BF16),
            pltpu.VMEM((NZ, 2 * GROUP, TOK), F32),
            pltpu.VMEM((NZ, 2 * GROUP, TOK), F32),
            pltpu.VMEM((8, TOK), F32),
            pltpu.VMEM((ROWS, NZ * TOK), BF16),
            pltpu.VMEM((NZ * TOK, ROWS), BF16),
            pltpu.VMEM((ROWS, TOK), BF16),
            pltpu.VMEM((NQ, NZ * TOK, DQ), BF16),
            pltpu.VMEM((NQ, ROWS, DQ), BF16),
            pltpu.VMEM((NQ, ROWS, DQ), BF16),
            pltpu.VMEM((NQ, ROWS, DQ), BF16),
            pltpu.VMEM((NQ, ROWS, DQ), BF16),
            pltpu.VMEM((NQ, ROWS, DQ), BF16),
            pltpu.VMEM((NQ, 2, 4, TOK, DQ), BF16),
            pltpu.VMEM((2, 2 * HID, D), BF16),
            pltpu.VMEM((2 * HID, D), BF16),
            pltpu.VMEM((2, 2 * ROWS, 2 * HID), F32),
            pltpu.VMEM((2 * ROWS, 2 * HID), BF16),
            dma((3,)), dma((3,)), dma((3,)),
            dma((2,)), dma((2,)), dma((2, 2)), dma((2, 2)), dma((NZ,)), dma((NZ,)),
            dma((NQ, 2, 4)), dma((NQ, 2, 4)), dma((NQ, GROUP)), dma((NQ, GROUP)), dma((NQ,)), dma((NQ,)),
            dma((NQ,)), dma((NQ,)), dma((NQ, GROUP)), dma((NQ, GROUP)), dma((NQ, 2, 4)), dma((NQ, 2, 4)),
        ],
        compiler_params=pltpu.CompilerParams(
            collective_id=0, has_side_effects=True, vmem_limit_bytes=60 * 2**20
        ),
        cost_estimate=pl.CostEstimate(flops=16 * 10**9, bytes_accessed=10**7, transcendentals=10**6),
    )(
        attn_heads, o_weight, resid, norm_gain[None, :], expert_ids.T, combine_weights.T,
        jnp.swapaxes(w_gate_up[0], 1, 2), w_down[0],
    )


def solution(mesh):
    in_specs = (
        P("expert", "tensor"),
        P("tensor", None),
        P(("expert", "tensor"), None),
        P(),
        P(("expert", "tensor"), None),
        P(("expert", "tensor"), None),
        P("expert", None, None, "tensor"),
        P("expert", "tensor", None),
    )
    out_specs = P(("expert", "tensor"), None)
    return jax.shard_map(
        on_device, mesh=mesh, in_specs=in_specs, out_specs=out_specs, check_vma=False
    )
```

```python
import functools

import jax
import jax.numpy as jnp
from jax import lax
from jax.experimental import pallas as pl
from jax.experimental.pallas import tpu as pltpu
from jax.sharding import PartitionSpec as P

MESH = pl.DeviceIdType.MESH
BF16 = jnp.bfloat16
F32 = jnp.float32
eps_norm = 1e-06

NZ, NY, NC, NX = 8, 4, 2, 4
GROUP = NY * NC
TOK = 128
D = 2048
CAP = 11
PIECE = 96
ROWS = GROUP * PIECE
HID = 352
NQ = 8
DQ = D // NQ
TILE = 384
YLAG = 2
XT, YT, ZT = 4, 4.5, 2
THEIR = (0, 0.5, 1, 2, 3, 3.5, 5, 6)
OUR = (1.5, 2.5, 5.5, 6.5, 9, 9.5, 13, 13.5)
PACE = 1


def nt(a, b):
    return lax.dot_general(a, b, (((1,), (1,)), ((), ())), preferred_element_type=F32)


def mm(a, b):
    return jnp.dot(a, b, preferred_element_type=F32)


PQ = 512


def pcols(q):
    return pl.ds(q * PQ, PQ)


def cols(q):
    return pl.ds(q * DQ, DQ)


def kernel(
    attn_in, ow_in, resid_in, gain, ids, wts, wgu_in, wd_in, out,
    attn, ow, resid, in_sem,
    mixed, far, nbr, far_in, nbr_in, meta_out, meta, vrow, gather, comb, gw,
    tok, ysend, yrecv, xrecv, xback, yback, zrecv, wgu, wd, acc, hidden,
    wl_sem, ws_sem, wr_sem, fs_sem, fr_sem, ns_sem, nr_sem, ms_sem, mr_sem,
    as_sem, ar_sem, ys_sem, yr_sem, xs_sem, xr_sem, bs_sem, br_sem, cs_sem, cr_sem, zs_sem, zr_sem,
):
    e = lax.axis_index("expert")
    x = lax.axis_index("tensor")
    z = e // GROUP
    y = (e // NC) % NY
    c = e % NC
    own_d = e % GROUP
    xr, xl = (x + 1) % NX, (x + NX - 1) % NX
    flip = x + 1 - 2 * (x % 2)
    mirror = NX - 1 - x
    wx = (1 - c) * mirror + c * flip
    px = (1 - c) * flip + c * mirror

    def at_z(dz):
        return (((z + dz + NZ) % NZ) * GROUP + own_d, x)

    def at_yc(j):
        return (z * GROUP + ((y + j // NC) % NY) * NC + (c + j % NC) % NC, x)

    def d_from(j):
        return ((y + NY - j // NC) % NY) * NC + (c + j % NC) % NC

    def d_to(j):
        return ((y + j // NC) % NY) * NC + (c + j % NC) % NC

    def rcopy(src, dst, send, recv, dev):
        return pltpu.make_async_remote_copy(
            src_ref=src, dst_ref=dst, send_sem=send, recv_sem=recv, device_id=dev, device_id_type=MESH
        )

    def landed(ref, sem):
        pltpu.make_async_copy(ref, ref, sem).wait()

    inputs = [
        pltpu.make_async_copy(attn_in, attn, in_sem.at[0]),
        pltpu.make_async_copy(ow_in, ow, in_sem.at[1]),
        pltpu.make_async_copy(resid_in, resid, in_sem.at[2]),
    ]
    wloc = [
        pltpu.make_async_copy(wgu_in.at[0], wgu.at[0, pl.ds(0, HID)], wl_sem.at[0]),
        pltpu.make_async_copy(wgu_in.at[1], wgu.at[1, pl.ds(0, HID)], wl_sem.at[1]),
        pltpu.make_async_copy(wd_in, wd.at[pl.ds(0, HID)], wl_sem.at[2]),
    ]
    for copy in inputs + wloc:
        copy.start()

    barrier = pltpu.get_barrier_semaphore()
    peers = [at_z(k) for k in range(1, NZ)] + [at_yc(j) for j in range(1, GROUP)] + [(e, xr), (e, xl)]
    for dev in peers:
        pl.semaphore_signal(barrier, inc=1, device_id=dev, device_id_type=MESH)
    pl.semaphore_wait(barrier, len(peers))

    inputs[0].wait()
    inputs[1].wait()

    def project(owner, q):
        return mm(attn[pl.ds(pl.multiple_of(owner * TOK, TOK), TOK), :], ow[:, pcols(q)])

    opposite = (x + 2) % NX
    far_copy = []
    for side in range(2):
        for q in (2 * side, 2 * side + 1):
            far[side, :, pl.ds((q % 2) * PQ, PQ)] = project(opposite, q).astype(BF16)
        far_copy.append(
            rcopy(far.at[side], far_in.at[side], fs_sem.at[side], fr_sem.at[side], (e, (xr, xl)[side]))
        )
        far_copy[-1].start()
    nbr_copy = []
    for side in range(2):
        part = 1 - side
        for q in (2 * part, 2 * part + 1):
            nbr[side, part, :, pl.ds((q % 2) * PQ, PQ)] = project((xr, xl)[side], q).astype(BF16)
        nbr_copy.append(
            rcopy(nbr.at[side, part], nbr_in.at[side, part], ns_sem.at[side, part], nr_sem.at[side, part], (e, (xr, xl)[side]))
        )
        nbr_copy[-1].start()
    for side in range(2):
        part = side
        for q in (2 * part, 2 * part + 1):
            mixed[:, pcols(q)] = project((xr, xl)[side], q)
        landed(far_in.at[side], fr_sem.at[side])
        for q in (2 * part, 2 * part + 1):
            at = pl.ds((q % 2) * PQ, PQ)
            nbr[side, part, :, at] = (mixed[:, pcols(q)] + far_in[side, :, at].astype(F32)).astype(BF16)
        nbr_copy.append(
            rcopy(nbr.at[side, part], nbr_in.at[side, part], ns_sem.at[side, part], nr_sem.at[side, part], (e, (xr, xl)[side]))
        )
        nbr_copy[-1].start()
    wrem = [
        rcopy(wgu_in.at[0], wgu.at[0, pl.ds(HID, HID)], ws_sem.at[0], wr_sem.at[0], (e, wx)),
        rcopy(wgu_in.at[1], wgu.at[1, pl.ds(HID, HID)], ws_sem.at[1], wr_sem.at[1], (e, wx)),
        rcopy(wd_in, wd.at[pl.ds(HID, HID)], ws_sem.at[2], wr_sem.at[2], (e, wx)),
    ]
    for copy in wrem:
        copy.start()

    inputs[2].wait()
    for q in range(4):
        mixed[:, pcols(q)] = project(x, q) + resid[:, pcols(q)].astype(F32)

    expert = lax.broadcasted_iota(jnp.int32, (NZ * GROUP, TOK), 0)
    holds = jnp.zeros((NZ * GROUP, TOK), F32)
    weight = jnp.zeros((NZ * GROUP, TOK), F32)
    for k in range(ids.shape[0]):
        named = expert == ids[k : k + 1, :]
        holds = holds + jnp.where(named, 1.0, 0.0)
        weight = weight + jnp.where(named, wts[k : k + 1, :], 0.0)
    before = lax.broadcasted_iota(jnp.int32, (TOK, TOK), 0) < lax.broadcasted_iota(jnp.int32, (TOK, TOK), 1)
    rank = mm(holds.astype(BF16), jnp.where(before, 1.0, 0.0).astype(BF16))
    place = jnp.where(holds > 0.5, rank + (z * CAP).astype(F32), -1.0)
    for p in range(NZ):
        meta_out[p, 0:GROUP, :] = place[p * GROUP : (p + 1) * GROUP, :]
        meta_out[p, GROUP : 2 * GROUP, :] = weight[p * GROUP : (p + 1) * GROUP, :]
    meta_copy = []
    for k in range(1, NZ):
        to = (z + k) % NZ
        meta_copy.append(rcopy(meta_out.at[to], meta.at[z], ms_sem.at[k], mr_sem.at[k], at_z(k)))
        meta_copy[-1].start()
    meta[z] = meta_out[z]

    for side in range(2):
        for part in range(2):
            landed(nbr_in.at[side, part], nr_sem.at[side, part])
            for q in (2 * part, 2 * part + 1):
                mixed[:, pcols(q)] = mixed[:, pcols(q)] + nbr_in[side, part, :, pl.ds((q % 2) * PQ, PQ)].astype(F32)

    square = jnp.zeros((TOK, 1), F32)
    for q in range(NQ):
        part = mixed[:, cols(q)]
        square = square + jnp.sum(part * part, axis=1, keepdims=True)
    scale = lax.rsqrt(square * (1.0 / D) + eps_norm)

    def hops(q):
        return (4, 3) if q % 2 == 0 else (3, 4)

    def block(s):
        return pl.ds(pl.multiple_of(s * TOK, TOK), TOK)

    sent = {}

    def ag_send(q, side, k):
        s = (z + NZ - (k - 1)) % NZ if side == 0 else (z + k - 1) % NZ
        ref = tok.at[q, block(s)]
        copy = rcopy(ref, ref, as_sem.at[q, side, k - 1], ar_sem.at[q, side, k - 1], at_z(1 if side == 0 else -1))
        copy.start()
        sent.setdefault(("ag", q), []).append(copy)

    def ag_start(q):
        tok[q, block(z), :] = (mixed[:, cols(q)] * scale * gain[:, cols(q)]).astype(BF16)
        for side in range(2):
            ag_send(q, side, 1)

    def ag_step(q, k):
        for side in range(2):
            if k > hops(q)[side]:
                continue
            s = (z + NZ - k) % NZ if side == 0 else (z + k) % NZ
            landed(tok.at[q, block(s)], ar_sem.at[q, side, k - 1])
            if k < hops(q)[side]:
                ag_send(q, side, k + 1)

    def piece(d):
        return pl.ds(pl.multiple_of(d * PIECE, 32), PIECE)

    def gather_step(q):
        def one(i, _):
            at = pl.ds(pl.multiple_of(i * TILE, TILE), TILE)
            ysend[q, at, :] = mm(gather[at, :], tok[q]).astype(BF16)
            return 0

        lax.fori_loop(0, ROWS // TILE, one, 0)
        for j in range(GROUP - 1, 0, -1):
            copy = rcopy(
                ysend.at[q, piece(d_to(j))], yrecv.at[q, piece(own_d)], ys_sem.at[q, j], yr_sem.at[q, j], at_yc(j)
            )
            copy.start()
            sent.setdefault(("y", q), []).append(copy)
        yrecv[q, piece(own_d), :] = ysend[q, piece(own_d), :]

    def share_step(q):
        for j in range(1, GROUP):
            landed(yrecv.at[q, piece(d_from(j))], yr_sem.at[q, j])
        copy = rcopy(yrecv.at[q], xrecv.at[q], xs_sem.at[q], xr_sem.at[q], (e, px))
        copy.start()
        sent[("x", q)] = [copy]

    def hidden_step(q, who):
        if q == 0 and who == 0:
            for copy in wloc:
                copy.wait()
            for i in range(2):
                landed(wgu.at[i, pl.ds(HID, HID)], wr_sem.at[i])
            landed(wd.at[pl.ds(HID, HID)], wr_sem.at[2])
        if who == 1:
            landed(xrecv.at[q], xr_sem.at[q])
        rows = (yrecv, xrecv)[who]

        def one(i, _):
            at = pl.ds(pl.multiple_of(i * TILE, TILE), TILE)
            to = pl.ds(pl.multiple_of(i * TILE + who * ROWS, TILE), TILE)
            lhs = rows[q, at, :]
            gate = nt(lhs, wgu[0, :, cols(q)])
            up = nt(lhs, wgu[1, :, cols(q)])
            if q > 0:
                gate = gate + acc[0, to, :]
                up = up + acc[1, to, :]
            if q < NQ - 1:
                acc[0, to, :] = gate
                acc[1, to, :] = up
            else:
                hidden[to, :] = (gate / (1.0 + jnp.exp(-gate)) * up).astype(BF16)
            return 0

        lax.fori_loop(0, ROWS // TILE, one, 0)

    def masks():
        for k in range(1, NZ):
            landed(meta.at[(z + NZ - k) % NZ], mr_sem.at[k])
        slot = lax.broadcasted_iota(jnp.int32, (PIECE, TOK), 0).astype(F32)
        eye = jnp.where(
            lax.broadcasted_iota(jnp.int32, (TOK, TOK), 0) == lax.broadcasted_iota(jnp.int32, (TOK, TOK), 1), 1.0, 0.0
        ).astype(BF16)
        for s in range(NZ):
            for d in range(GROUP):
                taken = slot == meta[s, d : d + 1, :]
                gather[d * PIECE : (d + 1) * PIECE, s * TOK : (s + 1) * TOK] = jnp.where(taken, 1.0, 0.0).astype(BF16)
                gw[d * PIECE : (d + 1) * PIECE, :] = jnp.where(
                    taken, meta[s, GROUP + d : GROUP + d + 1, :], 0.0
                ).astype(BF16)
            comb[s * TOK : (s + 1) * TOK, :] = nt(eye, gw[...]).astype(BF16)

    tasks = [(0, 9, masks)]
    for q in range(NQ):
        t = q * PACE
        tasks.append((t, 0, functools.partial(ag_start, q)))
        for k in range(1, 5):
            tasks.append((t + k, 1, functools.partial(ag_step, q, k)))
        tasks.append((t + 4, 2, functools.partial(gather_step, q)))
        tasks.append((t + 4 + YLAG, 3, functools.partial(share_step, q)))
        tasks.append((100 + q, 4, functools.partial(hidden_step, q, 0)))
        tasks.append((200 + q, 5, functools.partial(hidden_step, q, 1)))
    for task in sorted(tasks, key=lambda task: task[:2]):
        task[2]()

    def down_step(q, who):
        for copy in sent[("x", q)]:
            copy.wait_send()
        sent[("x", q)] = []

        def body(i, _):
            at = pl.ds(pl.multiple_of(i * TILE, TILE), TILE)
            of = pl.ds(pl.multiple_of(i * TILE + who * ROWS, TILE), TILE)
            (yrecv, xrecv)[who][q, at, :] = mm(hidden[of, :], wd[:, cols(q)]).astype(BF16)
            return 0

        lax.fori_loop(0, ROWS // TILE, body, 0)
        if who == 1:
            copy = rcopy(xrecv.at[q], xback.at[q], bs_sem.at[q], br_sem.at[q], (e, px))
            copy.start()
            sent[("b", q)] = [copy]

    def sum_step(q):
        landed(xback.at[q], br_sem.at[q])
        for copy in sent[("y", q)]:
            copy.wait_send()
        ysend[q] = (yrecv[q].astype(F32) + xback[q].astype(F32)).astype(BF16)
        for j in range(GROUP - 1, 0, -1):
            copy = rcopy(
                ysend.at[q, piece(d_to(j))], yback.at[q, piece(own_d)], cs_sem.at[q, j], cr_sem.at[q, j], at_yc(j)
            )
            copy.start()
            sent.setdefault(("c", q), []).append(copy)
        yback[q, piece(own_d), :] = ysend[q, piece(own_d), :]

    def rs_send(q, side, j):
        far_hops = hops(q)[side]
        k = far_hops + 1 - j
        s = (z + k) % NZ if side == 0 else (z + NZ - k) % NZ
        copy = rcopy(
            tok.at[q, block(s)], zrecv.at[q, side, j - 1], zs_sem.at[q, side, j - 1], zr_sem.at[q, side, j - 1],
            at_z(1 if side == 0 else -1),
        )
        copy.start()
        sent.setdefault(("z", q), []).append(copy)

    def combine_step(q):
        for j in range(1, GROUP):
            landed(yback.at[q, piece(d_from(j))], cr_sem.at[q, j])
        for copy in sent[("ag", q)]:
            copy.wait_send()

        def one(i, _):
            at = pl.ds(pl.multiple_of(i * 256, 256), 256)
            tok[q, at, :] = mm(comb[at, :], yback[q]).astype(BF16)
            return 0

        lax.fori_loop(0, NZ * TOK // 256, one, 0)
        for side in range(2):
            rs_send(q, side, 1)

    def rs_step(q, j):
        for side in range(2):
            far_hops = hops(q)[side]
            if j > far_hops:
                continue
            landed(zrecv.at[q, side, j - 1], zr_sem.at[q, side, j - 1])
            if j == far_hops:
                mixed[:, cols(q)] = mixed[:, cols(q)] + zrecv[q, side, j - 1].astype(F32)
                continue
            k = far_hops - j
            s = (z + k) % NZ if side == 0 else (z + NZ - k) % NZ
            tok[q, block(s), :] = (tok[q, block(s), :].astype(F32) + zrecv[q, side, j - 1].astype(F32)).astype(BF16)
            rs_send(q, side, j + 1)

    def finish(q):
        out[:, cols(q)] = (mixed[:, cols(q)] + tok[q, block(z), :].astype(F32)).astype(BF16)

    tasks = []
    for q in range(NQ):
        t = (q + 1) * XT
        tasks.append((OUR[q], 0, functools.partial(down_step, q, 0)))
        tasks.append((THEIR[q], 0, functools.partial(down_step, q, 1)))
        tasks.append((t, 1, functools.partial(sum_step, q)))
        tasks.append((t + YT, 2, functools.partial(combine_step, q)))
        for j in range(1, 5):
            tasks.append((t + YT + j * ZT, 3, functools.partial(rs_step, q, j)))
        tasks.append((t + YT + 4 * ZT, 4, functools.partial(finish, q)))
    for task in sorted(tasks, key=lambda task: task[:2]):
        task[2]()

    for copy in far_copy + nbr_copy + meta_copy + wrem:
        copy.wait_send()
    for q in range(NQ):
        for kind in ("b", "c", "z"):
            for copy in sent[(kind, q)]:
                copy.wait_send()


def on_device(
    attn_heads, o_weight, resid, norm_gain, expert_ids, combine_weights, w_gate_up, w_down
):
    vmem = pl.BlockSpec(memory_space=pltpu.VMEM)
    hbm = pl.BlockSpec(memory_space=pl.ANY)
    dma = pltpu.SemaphoreType.DMA
    return pl.pallas_call(
        kernel,
        out_shape=jax.ShapeDtypeStruct((TOK, D), BF16),
        in_specs=[hbm] * 3 + [vmem] * 3 + [hbm] * 2,
        out_specs=vmem,
        scratch_shapes=[
            pltpu.VMEM((4 * TOK, D // NX), BF16),
            pltpu.VMEM((D // NX, D), BF16),
            pltpu.VMEM((TOK, D), BF16),
            dma((3,)),
            pltpu.VMEM((TOK, D), F32),
            pltpu.VMEM((2, TOK, D // 2), BF16),
            pltpu.VMEM((2, 2, TOK, D // 2), BF16),
            pltpu.VMEM((2, TOK, D // 2), BF16),
            pltpu.VMEM((2, 2, TOK, D // 2), BF16),
            pltpu.VMEM((NZ, 2 * GROUP, TOK), F32),
            pltpu.VMEM((NZ, 2 * GROUP, TOK), F32),
            pltpu.VMEM((8, TOK), F32),
            pltpu.VMEM((ROWS, NZ * TOK), BF16),
            pltpu.VMEM((NZ * TOK, ROWS), BF16),
            pltpu.VMEM((ROWS, TOK), BF16),
            pltpu.VMEM((NQ, NZ * TOK, DQ), BF16),
            pltpu.VMEM((NQ, ROWS, DQ), BF16),
            pltpu.VMEM((NQ, ROWS, DQ), BF16),
            pltpu.VMEM((NQ, ROWS, DQ), BF16),
            pltpu.VMEM((NQ, ROWS, DQ), BF16),
            pltpu.VMEM((NQ, ROWS, DQ), BF16),
            pltpu.VMEM((NQ, 2, 4, TOK, DQ), BF16),
            pltpu.VMEM((2, 2 * HID, D), BF16),
            pltpu.VMEM((2 * HID, D), BF16),
            pltpu.VMEM((2, 2 * ROWS, 2 * HID), F32),
            pltpu.VMEM((2 * ROWS, 2 * HID), BF16),
            dma((3,)), dma((3,)), dma((3,)),
            dma((2,)), dma((2,)), dma((2, 2)), dma((2, 2)), dma((NZ,)), dma((NZ,)),
            dma((NQ, 2, 4)), dma((NQ, 2, 4)), dma((NQ, GROUP)), dma((NQ, GROUP)), dma((NQ,)), dma((NQ,)),
            dma((NQ,)), dma((NQ,)), dma((NQ, GROUP)), dma((NQ, GROUP)), dma((NQ, 2, 4)), dma((NQ, 2, 4)),
        ],
        compiler_params=pltpu.CompilerParams(
            collective_id=0, has_side_effects=True, vmem_limit_bytes=60 * 2**20
        ),
        cost_estimate=pl.CostEstimate(flops=16 * 10**9, bytes_accessed=10**7, transcendentals=10**6),
    )(
        attn_heads, o_weight, resid, norm_gain[None, :], expert_ids.T, combine_weights.T,
        jnp.swapaxes(w_gate_up[0], 1, 2), w_down[0],
    )


def solution(mesh):
    in_specs = (
        P("expert", "tensor"),
        P("tensor", None),
        P(("expert", "tensor"), None),
        P(),
        P(("expert", "tensor"), None),
        P(("expert", "tensor"), None),
        P("expert", None, None, "tensor"),
        P("expert", "tensor", None),
    )
    out_specs = P(("expert", "tensor"), None)
    return jax.shard_map(
        on_device, mesh=mesh, in_specs=in_specs, out_specs=out_specs, check_vma=False
    )
```
